512 devices in a mesh: dp: 32 (over z, core), dap: 16 (over x, y).
Axes of the slice: x: 4, y: 4, z: 16, core: 2. Of those that a mesh axis runs over, the one named last changes fastest.
Arguments:
- pair: bfloat16 [32, 192, 192, 128], P('dp', 'dap'), may hold values from -60 to 60
- pair_cot: bfloat16 [32, 192, 192, 128], P('dp', 'dap'), may hold values from -6 to 6
- residue_mask: int32 [32, 192], P('dp'), may hold values from 0 to 1, as said below
- w_in: bfloat16 [2, 128, 640], replicated, may hold values from -0.5 to 0.5
- w_out: bfloat16 [2, 128, 128], replicated, may hold values from -0.5 to 0.5
Outputs:
- pair_grad: bfloat16 [32, 192, 192, 128], P('dp', 'dap')
- w_in_grad: float32 [2, 128, 640], replicated
- w_out_grad: float32 [2, 128, 128], replicated
The draws below stay inside these ranges and needn't reach their ends.
Inputs may be any that keep to these rules, and one draw needn't show every extreme that they name: `residue_mask`: in each crop the real residues form a prefix of its 192 residues that holds at least half of them; the rest are 0.
All inputs are finite; a program needn't handle non-finite values.
Results may differ from the reference program's by a relative error of at most 0.019.
Values may be sent and summed in bfloat16 or wider, within the bound.
A program may use at most 192 MiB of HBM per device.

```python
import jax
import jax.numpy as jnp
from jax import lax

C = 128
H = 128
N = 192
CROPS = 32


def draw_pair(key, part):
    key = jax.random.fold_in(key, 11)
    base_key, cell_key, chan_key = jax.random.split(key, 3)
    shape = (CROPS, N, N, C)
    base = jnp.clip(jax.random.normal(base_key, shape, jnp.float32), -4.0, 4.0)
    spread = 1.15
    cell = jnp.exp(jax.random.uniform(cell_key, (CROPS, N, N, 1), jnp.float32, -spread, spread))
    channel = jnp.exp(jax.random.uniform(chan_key, (C,), jnp.float32, -spread, spread))
    return (base * cell * channel).astype(jnp.bfloat16)


def draw_residue_mask(key, part):
    key = jax.random.fold_in(key, 5)
    lengths = jax.random.randint(key, (CROPS, 1), N // 2, N + 1)
    positions = jnp.arange(N, dtype=jnp.int32)[None, :]
    return (positions < lengths).astype(jnp.int32)


def steps_of(stream_key, dims, shards, smallest, top_value):
    gain, own = 1.0, jax.random.fold_in(stream_key, 6)
    for dim, blocks in shards:
        draws = jnp.exp(jax.random.uniform(jax.random.fold_in(own, dim), (blocks,), jnp.float32, smallest / len(shards), top_value / len(shards)))
        gain = gain * jnp.repeat(draws, dims[dim] // blocks).reshape([-1 if axis == dim else 1 for axis in range(len(dims))])
    return gain


def noise(own_key, dims, scale, reach, cuts=(), held_as=jnp.bfloat16):
    array = jax.random.normal(own_key, dims, jnp.float32) * scale
    if len(cuts) > 0:
        array = steps_of(own_key, dims, cuts, -0.22, 0.18) * array
    return jnp.clip(array, min=-reach, max=reach).astype(held_as)


def setup_inputs(seed: int = 0) -> dict:
    keys = jax.random.split(jax.random.key(seed), 6)
    pair = draw_pair(jax.random.fold_in(keys[5], 71), 0)
    pair_cot = noise(keys[1], (CROPS, N, N, C), 1.0, 6.0, ((0, 32), (1, 16)))
    residue_mask = draw_residue_mask(jax.random.fold_in(keys[5], 71), 0)
    w_in = noise(keys[3], (2, C, 4 * H + C), C ** -0.5, 0.5)
    w_out = noise(keys[4], (2, H, C), H ** -0.5, 0.5)
    return {"pair": pair, "pair_cot": pair_cot, "residue_mask": residue_mask, "w_in": w_in, "w_out": w_out}


EPS = 1e-05

def normal_form(values):
    average = lax.optimization_barrier(jnp.mean(values, -1, keepdims=True))
    centred = values - average
    inv_std = lax.rsqrt(lax.optimization_barrier(jnp.mean(centred * centred, -1, keepdims=True)) + EPS)
    return (centred * inv_std, inv_std)

def norm_back(grad, normed, inv_std):
    return inv_std * (grad - lax.optimization_barrier(jnp.mean(grad, -1, keepdims=True)) - normed * lax.optimization_barrier(jnp.mean(grad * normed, -1, keepdims=True)))

def gated_pair(projected, pair_mask, hidden):
    left_value = projected[..., :hidden]
    left_gate = jax.nn.sigmoid(projected[..., hidden:2 * hidden])
    right_value = projected[..., 2 * hidden:3 * hidden]
    right_gate = jax.nn.sigmoid(projected[..., 3 * hidden:4 * hidden])
    left = (left_gate * left_value * pair_mask).astype(jnp.bfloat16)
    right = (right_gate * right_value * pair_mask).astype(jnp.bfloat16)
    return (left, right, (left_value, left_gate, right_value, right_gate))

def half_back(grad, value, gate, pair_mask):
    return jnp.concatenate([grad * gate * pair_mask, grad * value * pair_mask * gate * (1.0 - gate)], -1)

def matmul(first, second, form):
    return jnp.einsum(form, first.astype(jnp.float32), second.astype(jnp.float32))

def update_forward(pair_in, w_in, w_out, pair_mask, incoming):
    hidden = w_out.shape[0]
    split_at = 4 * hidden
    source = jnp.transpose(pair_in, (1, 0, 2)) if incoming else pair_in
    src_normed, src_inv = normal_form(source.astype(jnp.float32))
    src_zed = src_normed.astype(jnp.bfloat16)
    left, right, stored = gated_pair(matmul(src_zed, w_in[:, :split_at], 'ijc,cd->ijd'), pair_mask, hidden)
    own_normed, own_inv = normal_form(pair_in.astype(jnp.float32))
    own_zed = own_normed.astype(jnp.bfloat16)
    gate = jax.nn.sigmoid(matmul(own_zed, w_in[:, split_at:], 'ijc,cd->ijd'))
    tri = matmul(left, right, 'ikh,jkh->ijh')
    tri_normed, tri_inv = normal_form(tri)
    tri_zed = tri_normed.astype(jnp.bfloat16)
    result = matmul(tri_zed, w_out, 'ijh,hc->ijc')
    return (src_normed, src_inv, src_zed, left, right, stored, own_normed, own_inv, own_zed, gate, tri_normed, tri_inv, tri_zed, result)

def update_backward(upstream, saved, w_in, w_out, pair_mask, incoming):
    src_normed, src_inv, src_zed, left, right, stored, own_normed, own_inv, own_zed, gate, tri_normed, tri_inv, tri_zed, result = saved
    hidden = w_out.shape[0]
    split_at = 4 * hidden
    up_float = upstream.astype(jnp.float32)
    grad_result = (up_float * gate).astype(jnp.bfloat16)
    grad_gate = (up_float * result * gate * (1.0 - gate)).astype(jnp.bfloat16)
    grad_tri = norm_back(matmul(grad_result, w_out, 'ijc,hc->ijh'), tri_normed, tri_inv).astype(jnp.bfloat16)
    grad_left = matmul(grad_tri, right, 'ijh,jkh->ikh')
    grad_right = matmul(grad_tri, left, 'ijh,ikh->jkh')
    left_value, left_gate, right_value, right_gate = stored
    grad_proj = jnp.concatenate([half_back(grad_left, left_value, left_gate, pair_mask), half_back(grad_right, right_value, right_gate, pair_mask)], -1).astype(jnp.bfloat16)
    src_grad = norm_back(matmul(grad_proj, w_in[:, :split_at], 'ijd,cd->ijc'), src_normed, src_inv)
    if incoming:
        src_grad = jnp.transpose(src_grad, (1, 0, 2))
    own_grad = norm_back(matmul(grad_gate, w_in[:, split_at:], 'ijd,cd->ijc'), own_normed, own_inv)
    new_upstream = (up_float + own_grad + src_grad).astype(jnp.bfloat16)
    in_grad = jnp.concatenate([matmul(src_zed, grad_proj, 'ijc,ijd->cd'), matmul(own_zed, grad_gate, 'ijc,ijd->cd')], 1)
    out_grad = matmul(tri_zed, grad_result, 'ijh,ijc->hc')
    return (new_upstream, in_grad, out_grad)

def reference(pair, pair_cot, residue_mask, w_in, w_out):

    def crop_grads(inputs):
        crop_pair, crop_cot, crop_valid = inputs
        residues = crop_valid.astype(jnp.float32)
        pair_mask = (residues[:, None] * residues[None, :])[:, :, None]
        saved_one = update_forward(crop_pair, w_in[0], w_out[0], pair_mask, False)
        pair_two = (crop_pair.astype(jnp.float32) + saved_one[9] * saved_one[13]).astype(jnp.bfloat16)
        saved_two = update_forward(pair_two, w_in[1], w_out[1], pair_mask, True)
        upstream, in_two, out_two = update_backward(crop_cot, saved_two, w_in[1], w_out[1], pair_mask, True)
        crop_grad, in_one, out_one = update_backward(upstream, saved_one, w_in[0], w_out[0], pair_mask, False)
        return (crop_grad, jnp.stack([in_one, in_two]), jnp.stack([out_one, out_two]))
    pair_grad, in_all, out_all = lax.map(crop_grads, (pair, pair_cot, residue_mask))
    length = pair.shape[1]
    return (pair_grad, lax.optimization_barrier(jnp.sum(in_all, 0)) / length, lax.optimization_barrier(jnp.sum(out_all, 0)) / length)
```

```python
import functools

import jax
import jax.numpy as jnp
from jax import lax
from jax.experimental import pallas as pl
from jax.experimental.pallas import tpu as pltpu
from jax.sharding import PartitionSpec as P

EPS = 1e-05
D = 16
R = 12
N = 192
C = 128
CH = 6
W = 2 * N
ROWS = 5 * C + C
PART = ROWS // D
f32 = jnp.float32
bf16 = jnp.bfloat16
MESH = pl.DeviceIdType.MESH


def dot(a, b, ca, cb):
    return lax.dot_general(a, b, (((ca,), (cb,)), ((), ())), preferred_element_type=f32)


def normal_form(x):
    centred = x - jnp.mean(x, 0, keepdims=True)
    inv = lax.rsqrt(jnp.mean(centred * centred, 0, keepdims=True) + EPS)
    return centred * inv, inv


def norm_back(d, n, inv):
    return inv * (d - jnp.mean(d, 0, keepdims=True) - n * jnp.mean(d * n, 0, keepdims=True))


def kernel(
    ndp,
    pair_ref, cot_ref, mask_ref, wt_ref, wp_ref, wo_ref, wot_ref,
    out_ref, gin_ref, gout_ref,
    n_ref, inv_ref, z_ref, v_ref, sg_ref, gate_ref, res_ref, ntri_ref, itri_ref, xz_ref,
    p_ref, up_ref, dres_ref, dq_ref, lm_ref, tm_ref, a_ref, b_ref,
    big_send, small_send, big_recv, small_recv,
    grads, rs_recv, dp_send, dp_recv, dp_all, fin_all,
    ssem, rsem, lsem, dps, dpr,
):
    me = lax.axis_index("dap")
    my = lax.axis_index("dp")

    barrier = pltpu.get_barrier_semaphore()

    @pl.loop(1, D)
    def _(k):
        pl.semaphore_signal(barrier, inc=1, device_id={"dap": lax.rem(me + k, D)}, device_id_type=MESH)

    @pl.loop(1, ndp)
    def _(k):
        pl.semaphore_signal(barrier, inc=1, device_id={"dp": lax.rem(my + k, ndp)}, device_id_type=MESH)

    count = jnp.sum(mask_ref[...].astype(f32), 1, keepdims=True)

    def cell_mask(c):
        lane = lax.broadcasted_iota(jnp.int32, (1, W), 1)
        second = ((lane >= C) & (lane < 2 * C)) | (lane >= 2 * C + 64)
        k = jnp.where(lane < C, lane, jnp.where(lane < 2 * C + 64, lane - C, lane - N))
        k = jnp.where((lane >= C) & (lane < 2 * C), lane - C, k)
        row = me * R + 2 * c + second.astype(jnp.int32)
        return jnp.where((jnp.maximum(k, row).astype(f32) < count), 1.0, 0.0).astype(f32)

    def load_cells(ref, c):
        i = 2 * c
        x = jnp.concatenate(
            [ref[i, 0:C], ref[i + 1, 0:C], ref[i, C:N], ref[i + 1, C:N]], 0
        )
        return jnp.transpose(x.astype(f32))

    def copy_of(send, recv, phase, peer, slot, src):
        return pltpu.make_async_remote_copy(
            src_ref=send.at[peer],
            dst_ref=recv.at[slot],
            send_sem=ssem.at[phase, peer],
            recv_sem=rsem.at[phase, src],
            device_id={"dap": peer},
            device_id_type=MESH,
        )

    def send_to(send, recv, phase, peer):
        copy_of(send, recv, phase, peer, me, me).start()

    def own_copy(send, recv):
        return pltpu.make_async_copy(send.at[me], recv.at[me], lsem)

    def wait_from(send, recv, phase, src):
        copy_of(send, recv, phase, src, src, src).wait_recv()

    def send_all(send, recv, phase):
        own_copy(send, recv).start()

        @pl.loop(1, D)
        def _(k):
            send_to(send, recv, phase, lax.rem(me + k, D))

    def wait_sends(send, recv, phase):
        @pl.loop(1, D)
        def _(k):
            copy_of(send, recv, phase, lax.rem(me + k, D), me, me).wait_send()

    def wait_all(send, recv, phase):
        own_copy(send, recv).wait()

        @pl.loop(1, D)
        def _(k):
            wait_from(send, recv, phase, lax.rem(me + D - k, D))

    def project(u, c, x):
        n, inv = normal_form(x)
        n_ref[u, c] = n
        inv_ref[u, c] = inv
        z = n.astype(bf16)
        z_ref[u, c] = z
        mask = cell_mask(c)
        for g in range(2):
            v = dot(wt_ref[u, g * C : (g + 1) * C], z, 1, 0)
            sg = jax.nn.sigmoid(dot(wt_ref[u, (2 + g) * C : (3 + g) * C], z, 1, 0))
            v_ref[u, c, g * C : (g + 1) * C] = v
            sg_ref[u, c, g * C : (g + 1) * C] = sg
            lr = (sg * v * mask).astype(bf16)
            big_send[g * 8 : (g + 1) * 8, c] = lr.reshape(8, 16, W)
        gate_ref[u, c] = jax.nn.sigmoid(dot(wt_ref[u, 4 * C : 5 * C], z, 1, 0))

    def finish_product(u, c, t):
        n, inv = normal_form(t)
        ntri_ref[u, c] = n
        itri_ref[u, c] = inv
        xz = n.astype(bf16)
        xz_ref[u, c] = xz
        res = dot(wot_ref[u], xz, 1, 0)
        res_ref[u, c] = res
        return res

    def back_to_product(u, c, up):
        gate = gate_ref[u, c]
        dres = (up * gate).astype(bf16)
        dres_ref[u, c] = dres
        dq_ref[u, c, 4 * C : 5 * C] = (up * res_ref[u, c] * gate * (1.0 - gate)).astype(bf16)
        return norm_back(dot(wo_ref[u], dres, 1, 0), ntri_ref[u, c], itri_ref[u, c])

    def back_to_pair(u, c, slot):
        mask = cell_mask(c)
        for g in range(2):
            d = big_recv[slot, g * 8 : (g + 1) * 8, c].reshape(C, W).astype(f32)
            sg = sg_ref[u, c, g * C : (g + 1) * C]
            dv = d * sg * mask
            dq_ref[u, c, g * C : (g + 1) * C] = dv.astype(bf16)
            dg = dv * v_ref[u, c, g * C : (g + 1) * C] * (1.0 - sg)
            dq_ref[u, c, (2 + g) * C : (3 + g) * C] = dg.astype(bf16)
        d = dot(wp_ref[u], dq_ref[u, c], 1, 0)
        return norm_back(d, n_ref[u, c], inv_ref[u, c])

    def halves(slot, p):
        x = small_recv[slot, :, p].astype(f32).reshape(D, 2, 8, W)
        return x[:, 0].reshape(C, W), x[:, 1].reshape(C, W)

    def put_halves(p, pieces):
        both = [y.reshape(D, 1, 8, W) for y in pieces]
        small_send[:, p] = jnp.concatenate(both, 1).reshape(D, 16, W).astype(bf16)

    def in_grad(u):
        def step(c, acc):
            return acc + dot(dq_ref[u, c], z_ref[u, c], 1, 1)

        acc = lax.fori_loop(0, CH, step, jnp.zeros((5 * C, C), f32))
        for k in range(5 * C // 16):
            r = k * 16
            grads[r // PART, u, r % PART : r % PART + 16] = acc[r : r + 16]

    def out_grad(u):
        def step(c, acc):
            return acc + dot(xz_ref[u, c], dres_ref[u, c], 1, 1)

        acc = lax.fori_loop(0, CH, step, jnp.zeros((C, C), f32))
        for k in range(C // 16):
            r = 5 * C + k * 16
            grads[r // PART, u, r % PART : r % PART + 16] = acc[k * 16 : k * 16 + 16]

    def spread(x, row, step):
        a_ref[pl.ds(row, step)] = x[:, 0:C]
        a_ref[pl.ds(row + step, step)] = x[:, C : 2 * C]
        tail = x[:, 2 * C : W]
        b_ref[pl.ds(row, step)] = tail
        b_ref[pl.ds(row + step, step)] = pltpu.roll(tail, 64, 1)

    def collect(row, step):
        lane = lax.broadcasted_iota(jnp.int32, (step, C), 1)
        tail = jnp.where(lane < 64, b_ref[pl.ds(row, step)], b_ref[pl.ds(row + step, step)])
        return jnp.concatenate([a_ref[pl.ds(row, step)], a_ref[pl.ds(row + step, step)], tail], 1)

    def get_channel(ch, step):
        a = a_ref[pl.ds(ch, N, stride=step), :]
        b = b_ref[pl.ds(ch, N, stride=step), :]
        return a.astype(bf16), b[:, :64].astype(bf16)

    def put_channel(ch, step, x):
        a_ref[pl.ds(ch, N, stride=step), :] = x[:, 0:C]
        b_ref[pl.ds(ch, N, stride=step), :] = jnp.concatenate([x[:, C:N], x[:, C:N]], 1)

    def arrive(send, recv, phase, k):
        src = lax.rem(me + D - k, D)

        @pl.when(k == 0)
        def _():
            own_copy(send, recv).wait()

        @pl.when(k > 0)
        def _():
            wait_from(send, recv, phase, src)

        return src

    def depart(send, recv, phase, k):
        peer = lax.rem(me + k, D)

        @pl.when(k == 0)
        def _():
            own_copy(send, recv).start()

        @pl.when(k > 0)
        def _():
            send_to(send, recv, phase, peer)

    def products(u, phase, slot):
        recv = big_recv.at[slot]

        @pl.loop(0, D)
        def _(k):
            src = arrive(big_send, recv, phase, k)
            for c in range(CH):
                spread(big_recv[slot, src, c].astype(f32), (src * R + 2 * c) * 16, 16)

        for ch in range(16):
            a, b = get_channel(ch, 16)
            lm_ref[u, ch, :, 0:C] = a
            lm_ref[u, ch, :, C:N] = b
        for ch in range(8):
            left, right = lm_ref[u, ch], lm_ref[u, 8 + ch]
            axis = 1 - u
            put_channel(ch, 8, dot(left, right, axis, axis))

        @pl.loop(0, D)
        def _(k):
            peer = lax.rem(me + k, D)
            for p in range(CH // 2):
                row = (peer * R + 4 * p) * 8
                both = jnp.concatenate([collect(row, 8), collect(row + 16, 8)], 0)
                small_send[peer, p] = both.astype(bf16)
            depart(small_send, small_recv.at[slot], phase + 1, k)

    def product_grads(u, phase, slot):
        recv = small_recv.at[slot]

        @pl.loop(0, D)
        def _(k):
            src = arrive(small_send, recv, phase, k)
            for p in range(CH // 2):
                x = small_recv[slot, src, p].astype(f32)
                row = (src * R + 4 * p) * 8
                spread(x[0:8], row, 8)
                spread(x[8:16], row + 16, 8)

        for ch in range(8):
            a, b = get_channel(ch, 8)
            tm_ref[ch, :, 0:C] = a
            tm_ref[ch, :, C:N] = b
        for ch in range(8):
            left, right, grad = lm_ref[u, ch], lm_ref[u, 8 + ch], tm_ref[ch]
            if u == 0:
                dleft, dright = dot(grad, right, 1, 0), dot(grad, left, 0, 0)
            else:
                dleft, dright = dot(right, grad, 1, 1), dot(left, grad, 1, 0)
            put_channel(ch, 16, dleft)
            put_channel(8 + ch, 16, dright)

        @pl.loop(0, D)
        def _(k):
            peer = lax.rem(me + k, D)
            for c in range(CH):
                big_send[peer, c] = collect((peer * R + 2 * c) * 16, 16).astype(bf16)
            depart(big_send, big_recv.at[slot], phase + 1, k)

    @pl.loop(0, CH)
    def _(c):
        project(0, c, load_cells(pair_ref, c))

    pl.semaphore_wait(barrier, D - 1 + ndp - 1)
    send_all(big_send, big_recv.at[0], 0)
    products(0, 0, 0)
    wait_sends(big_send, big_recv.at[0], 0)
    wait_all(small_send, small_recv.at[0], 1)

    @pl.loop(0, CH // 2)
    def _(p):
        for a, t in enumerate(halves(0, p)):
            c = 2 * p + a
            res = finish_product(0, c, t)
            one = (load_cells(pair_ref, c) + gate_ref[0, c] * res).astype(bf16)
            project(1, c, one.astype(f32))

    send_all(big_send, big_recv.at[1], 2)
    wait_sends(small_send, small_recv.at[0], 1)
    products(1, 2, 1)
    wait_sends(big_send, big_recv.at[1], 2)
    wait_all(small_send, small_recv.at[1], 3)
    wait_sends(small_send, small_recv.at[1], 3)

    @pl.loop(0, CH // 2)
    def _(p):
        pieces = []
        for a, t in enumerate(halves(1, p)):
            c = 2 * p + a
            finish_product(1, c, t)
            pieces.append(back_to_product(1, c, load_cells(cot_ref, c)))
        put_halves(p, pieces)

    send_all(small_send, small_recv.at[2], 4)
    out_grad(1)
    product_grads(1, 4, 2)
    wait_sends(small_send, small_recv.at[2], 4)
    wait_all(big_send, big_recv.at[2], 5)

    @pl.loop(0, CH // 2)
    def _(p):
        pieces = []
        for a in range(2):
            c = 2 * p + a
            up = load_cells(cot_ref, c) + back_to_pair(1, c, 2)
            up = up.astype(bf16)
            up_ref[c] = up
            pieces.append(back_to_product(0, c, up.astype(f32)))
        put_halves(p, pieces)

    send_all(small_send, small_recv.at[3], 6)
    wait_sends(big_send, big_recv.at[2], 5)
    in_grad(1)
    out_grad(0)
    product_grads(0, 6, 3)
    wait_sends(small_send, small_recv.at[3], 6)
    wait_all(big_send, big_recv.at[3], 7)

    @pl.loop(0, CH)
    def _(c):
        total = up_ref[c].astype(f32) + back_to_pair(0, c, 3)
        y = jnp.transpose(total).astype(bf16)
        i = 2 * c
        out_ref[i, 0:C] = y[0:C]
        out_ref[i + 1, 0:C] = y[C : 2 * C]
        out_ref[i, C:N] = y[2 * C : 2 * C + 64]
        out_ref[i + 1, C:N] = y[2 * C + 64 : W]

    in_grad(0)
    wait_sends(big_send, big_recv.at[3], 7)

    send_all(grads, rs_recv, 8)
    wait_all(grads, rs_recv, 8)

    def add(k, acc):
        return acc + rs_recv[k].reshape(2 * PART, C)

    total = lax.fori_loop(1, D, add, rs_recv[0].reshape(2 * PART, C))
    piece = 2 * PART // ndp
    for k in range(ndp):
        dp_send[k] = total[k * piece : (k + 1) * piece]

    def dp_copy(src, dst, stage, peer, slot, origin):
        return pltpu.make_async_remote_copy(
            src_ref=src,
            dst_ref=dst.at[slot],
            send_sem=dps.at[stage, peer],
            recv_sem=dpr.at[stage, origin],
            device_id={"dp": peer},
            device_id_type=MESH,
        )

    @pl.loop(1, ndp)
    def _(k):
        peer = lax.rem(my + k, ndp)
        dp_copy(dp_send.at[peer], dp_recv, 0, peer, my, my).start()

    dp_recv[my] = dp_send[my]

    @pl.loop(1, ndp)
    def _(k):
        peer = lax.rem(my + ndp - k, ndp)
        dp_copy(dp_send.at[peer], dp_recv, 0, peer, peer, peer).wait_recv()

    acc = dp_recv[0]
    for k in range(1, ndp):
        acc = acc + dp_recv[k]
    dp_all[my] = acc

    @pl.loop(1, ndp)
    def _(k):
        peer = lax.rem(my + k, ndp)
        dp_copy(dp_all.at[my], dp_all, 1, peer, my, my).start()

    @pl.loop(1, ndp)
    def _(k):
        peer = lax.rem(my + ndp - k, ndp)
        dp_copy(dp_all.at[peer], dp_all, 1, peer, peer, peer).wait_recv()

    whole = jnp.concatenate([dp_all[k] for k in range(ndp)], 0)
    fin_all[me] = (whole * (1.0 / N)).reshape(2, PART, C)

    def fin_copy(peer, slot):
        return pltpu.make_async_remote_copy(
            src_ref=fin_all.at[slot],
            dst_ref=fin_all.at[slot],
            send_sem=ssem.at[9, peer],
            recv_sem=rsem.at[9, slot],
            device_id={"dap": peer},
            device_id_type=MESH,
        )

    @pl.loop(1, D)
    def _(k):
        fin_copy(lax.rem(me + k, D), me).start()

    @pl.loop(1, D)
    def _(k):
        peer = lax.rem(me + D - k, D)
        fin_copy(peer, peer).wait_recv()

    for u in range(2):
        full = fin_all[:, u].reshape(ROWS, C)
        for t in range(2):
            part = full[t * 2 * C : (t + 1) * 2 * C].reshape(D, 2, 8, C)
            for s in range(2):
                at = (2 * s + t) * C
                gin_ref[u, :, at : at + C] = jnp.transpose(part[:, s].reshape(C, C))
        gin_ref[u, :, 4 * C : 5 * C] = jnp.transpose(full[4 * C : 5 * C])
        gout_ref[u] = full[5 * C : ROWS]

    wait_sends(grads, rs_recv, 8)

    @pl.loop(1, ndp)
    def _(k):
        peer = lax.rem(my + k, ndp)
        dp_copy(dp_send.at[peer], dp_recv, 0, peer, my, my).wait_send()
        dp_copy(dp_all.at[my], dp_all, 1, peer, my, my).wait_send()

    @pl.loop(1, D)
    def _(k):
        fin_copy(lax.rem(me + k, D), me).wait_send()


def local(ndp, pair, pair_cot, residue_mask, w_in, w_out):
    cols = w_in[..., : 4 * C].reshape(2, C, 2, 2, D, 8).transpose(0, 1, 3, 4, 2, 5).reshape(2, C, 4 * C)
    wp = jnp.concatenate([cols, w_in[..., 4 * C :]], -1)
    wt = jnp.swapaxes(wp, 1, 2)
    wot = jnp.swapaxes(w_out, 1, 2)
    vmem = pl.BlockSpec(memory_space=pltpu.VMEM)
    piece = 2 * PART // ndp
    scratch = [
        pltpu.VMEM((2, CH, C, W), f32),
        pltpu.VMEM((2, CH, 1, W), f32),
        pltpu.VMEM((2, CH, C, W), bf16),
        pltpu.VMEM((2, CH, 2 * C, W), f32),
        pltpu.VMEM((2, CH, 2 * C, W), f32),
        pltpu.VMEM((2, CH, C, W), f32),
        pltpu.VMEM((2, CH, C, W), f32),
        pltpu.VMEM((2, CH, C, W), f32),
        pltpu.VMEM((2, CH, 1, W), f32),
        pltpu.VMEM((2, CH, C, W), bf16),
        pltpu.VMEM((8, C), f32),
        pltpu.VMEM((CH, C, W), bf16),
        pltpu.VMEM((2, CH, C, W), bf16),
        pltpu.VMEM((2, CH, 5 * C, W), bf16),
        pltpu.VMEM((2, 16, N, N), bf16),
        pltpu.VMEM((8, N, N), bf16),
        pltpu.VMEM((N * 16, C), f32),
        pltpu.VMEM((N * 16, C), f32),
        pltpu.VMEM((D, CH, 16, W), bf16),
        pltpu.VMEM((D, CH // 2, 16, W), bf16),
        pltpu.VMEM((4, D, CH, 16, W), bf16),
        pltpu.VMEM((4, D, CH // 2, 16, W), bf16),
        pltpu.VMEM((D, 2, PART, C), f32),
        pltpu.VMEM((D, 2, PART, C), f32),
        pltpu.VMEM((ndp, piece, C), f32),
        pltpu.VMEM((ndp, piece, C), f32),
        pltpu.VMEM((ndp, piece, C), f32),
        pltpu.VMEM((D, 2, PART, C), f32),
        pltpu.SemaphoreType.DMA((10, D)),
        pltpu.SemaphoreType.DMA((10, D)),
        pltpu.SemaphoreType.DMA,
        pltpu.SemaphoreType.DMA((2, ndp)),
        pltpu.SemaphoreType.DMA((2, ndp)),
    ]
    grad, in_total, out_total = pl.pallas_call(
        functools.partial(kernel, ndp),
        out_shape=(
            jax.ShapeDtypeStruct((R, N, C), bf16),
            jax.ShapeDtypeStruct((2, C, 5 * C), f32),
            jax.ShapeDtypeStruct((2, C, C), f32),
        ),
        in_specs=[vmem] * 7,
        out_specs=(vmem, vmem, vmem),
        scratch_shapes=scratch,
        compiler_params=pltpu.CompilerParams(
            collective_id=0, has_side_effects=True, vmem_limit_bytes=60 * 1024 * 1024
        ),
    )(pair[0], pair_cot[0], residue_mask, wt, wp, w_out, wot)
    return grad[None], in_total, out_total


def solution(mesh):
    return jax.shard_map(
        functools.partial(local, mesh.shape["dp"]),
        mesh=mesh,
        in_specs=(P("dp", "dap", None, None), P("dp", "dap", None, None), P("dp", None), P(), P()),
        out_specs=(P("dp", "dap", None, None), P(), P()),
        check_vma=False,
    )
```

```python
import functools

import jax
import jax.numpy as jnp
from jax import lax
from jax.experimental import pallas as pl
from jax.experimental.pallas import tpu as pltpu
from jax.sharding import PartitionSpec as P

EPS = 1e-05
D = 16
R = 12
N = 192
C = 128
CH = 6
W = 2 * N
CELLS = R * N
EARLY = 8 * C
LATE = 4 * C
f32 = jnp.float32
bf16 = jnp.bfloat16
MESH = pl.DeviceIdType.MESH


def dot(a, b, ca, cb):
    return lax.dot_general(a, b, (((ca,), (cb,)), ((), ())), preferred_element_type=f32)


def normal_form(x):
    centred = x - jnp.mean(x, 0, keepdims=True)
    inv = lax.rsqrt(jnp.mean(centred * centred, 0, keepdims=True) + EPS)
    return centred * inv, inv


def norm_back(d, n, inv):
    return inv * (d - jnp.mean(d, 0, keepdims=True) - n * jnp.mean(d * n, 0, keepdims=True))


def kernel(
    ndp,
    pair_ref, cot_ref, mask_ref, win_ref, wo_ref,
    out_ref, gin_ref, gout_ref,
    wt_ref, wp_ref, wot_ref,
    n_ref, inv_ref, z_ref, v_ref, sg_ref, gate_ref, res_ref, ntri_ref, itri_ref, xz_ref,
    up_ref, dres_ref, dq_ref, lm_ref, tm_ref, a_ref, b_ref,
    big_send, small_send, big_recv, small_recv,
    early, late, early_in, late_in, half_out, half_in, z_early, z_late, early_all, late_all,
    ssem, rsem, lsem, core_s, core_r, zs, zr,
):
    me = lax.axis_index("dap")
    my = lax.axis_index("dp")
    core, zed, nz = lax.rem(my, 2), my // 2, ndp // 2
    mate = my + 1 - 2 * core

    def offset(k, sign):
        j = lax.rem(7 * k, D)
        a, b = j // 4, lax.rem(j, 4)
        dx, dy = a + core * (b - a), b + core * (a - b)
        return lax.rem(me // 4 + 4 + sign * dx, 4) * 4 + lax.rem(lax.rem(me, 4) + 4 + sign * dy, 4)

    def peer_of(k):
        return offset(k, 1)

    def src_of(k):
        return offset(k, -1)

    def z_peer(k):
        return 2 * lax.rem(zed + k, nz) + core

    barrier = pltpu.get_barrier_semaphore()

    @pl.loop(1, D)
    def _(k):
        pl.semaphore_signal(barrier, inc=1, device_id={"dap": peer_of(k)}, device_id_type=MESH)

    pl.semaphore_signal(barrier, inc=1, device_id={"dp": mate}, device_id_type=MESH)

    @pl.loop(1, nz)
    def _(k):
        pl.semaphore_signal(barrier, inc=1, device_id={"dp": z_peer(k)}, device_id_type=MESH)

    for u in range(2):
        wt = jnp.transpose(win_ref[u].astype(f32))
        pieces = []
        for t in range(2):
            both = [wt[(2 * e + t) * C : (2 * e + t + 1) * C].reshape(D, 1, 8, C) for e in range(2)]
            pieces.append(jnp.concatenate(both, 1).reshape(2 * C, C))
        wt = jnp.concatenate(pieces + [wt[4 * C : 5 * C]], 0)
        wt_ref[u] = wt.astype(bf16)
        wp_ref[u] = jnp.transpose(wt).astype(bf16)
        wot_ref[u] = jnp.transpose(wo_ref[u].astype(f32)).astype(bf16)

    count = jnp.sum(mask_ref[...].astype(f32), 1, keepdims=True)

    def cell_mask(c):
        lane = lax.broadcasted_iota(jnp.int32, (1, W), 1)
        second = ((lane >= C) & (lane < 2 * C)) | (lane >= 2 * C + 64)
        k = jnp.where(lane < C, lane, jnp.where(lane < 2 * C + 64, lane - C, lane - N))
        k = jnp.where((lane >= C) & (lane < 2 * C), lane - C, k)
        row = me * R + 2 * c + second.astype(jnp.int32)
        return jnp.where((jnp.maximum(k, row).astype(f32) < count), 1.0, 0.0).astype(f32)

    def cells(c):
        return pl.ds(pl.multiple_of(c * W, C), W)

    def load_cells(ref, c):
        i = 2 * c
        x = jnp.concatenate(
            [ref[i, 0:C], ref[i + 1, 0:C], ref[i, C:N], ref[i + 1, C:N]], 0
        )
        return jnp.transpose(x.astype(f32))

    def copy_of(send, recv, phase, peer, slot, src):
        return pltpu.make_async_remote_copy(
            src_ref=send.at[peer],
            dst_ref=recv.at[slot],
            send_sem=ssem.at[phase, peer],
            recv_sem=rsem.at[phase, src],
            device_id={"dap": peer},
            device_id_type=MESH,
        )

    def send_to(send, recv, phase, peer):
        copy_of(send, recv, phase, peer, me, me).start()

    def own_copy(send, recv, phase):
        return pltpu.make_async_copy(send.at[me], recv.at[me], lsem.at[phase])

    def wait_from(send, recv, phase, src):
        copy_of(send, recv, phase, src, src, src).wait_recv()

    def send_all(send, recv, phase):
        own_copy(send, recv, phase).start()

        @pl.loop(1, D)
        def _(k):
            send_to(send, recv, phase, peer_of(k))

    def wait_sends(send, recv, phase):
        @pl.loop(1, D)
        def _(k):
            copy_of(send, recv, phase, peer_of(k), me, me).wait_send()

    def wait_all(send, recv, phase):
        own_copy(send, recv, phase).wait()

        @pl.loop(1, D)
        def _(k):
            wait_from(send, recv, phase, src_of(k))

    def project(u, c, x):
        n, inv = normal_form(x)
        n_ref[u, c] = n
        inv_ref[u, c] = inv
        z = n.astype(bf16)
        z_ref[u, :, cells(c)] = z
        mask = cell_mask(c)
        for g in range(2):
            v = dot(wt_ref[u, g * C : (g + 1) * C], z, 1, 0)
            sg = jax.nn.sigmoid(dot(wt_ref[u, (2 + g) * C : (3 + g) * C], z, 1, 0))
            v_ref[u, c, g * C : (g + 1) * C] = v
            sg_ref[u, c, g * C : (g + 1) * C] = sg
            lr = (sg * v * mask).astype(bf16)
            big_send[g * 8 : (g + 1) * 8, c] = lr.reshape(8, 16, W)
        gate_ref[u, c] = jax.nn.sigmoid(dot(wt_ref[u, 4 * C : 5 * C], z, 1, 0))

    def finish_product(u, c, t):
        n, inv = normal_form(t)
        ntri_ref[u, c] = n
        itri_ref[u, c] = inv
        xz = n.astype(bf16)
        xz_ref[u, :, cells(c)] = xz
        res = dot(wot_ref[u], xz, 1, 0)
        res_ref[u, c] = res
        return res

    def back_to_product(u, c, up):
        gate = gate_ref[u, c]
        dres = (up * gate).astype(bf16)
        dres_ref[u, :, cells(c)] = dres
        dq_ref[u, 4 * C : 5 * C, cells(c)] = (up * res_ref[u, c] * gate * (1.0 - gate)).astype(bf16)
        return norm_back(dot(wo_ref[u], dres, 1, 0), ntri_ref[u, c], itri_ref[u, c])

    def back_to_factors(u, c, slot):
        mask = cell_mask(c)
        for g in range(2):
            d = big_recv[slot, g * 8 : (g + 1) * 8, c].reshape(C, W).astype(f32)
            sg = sg_ref[u, c, g * C : (g + 1) * C]
            dv = d * sg * mask
            dq_ref[u, g * C : (g + 1) * C, cells(c)] = dv.astype(bf16)
            dg = dv * v_ref[u, c, g * C : (g + 1) * C] * (1.0 - sg)
            dq_ref[u, (2 + g) * C : (3 + g) * C, cells(c)] = dg.astype(bf16)

    def back_to_pair(u, c):
        d = dot(wp_ref[u], dq_ref[u, :, cells(c)], 1, 0)
        return norm_back(d, n_ref[u, c], inv_ref[u, c])

    def halves(slot, p):
        x = small_recv[slot, :, p].astype(f32).reshape(D, 2, 8, W)
        return x[:, 0].reshape(C, W), x[:, 1].reshape(C, W)

    def put_halves(p, pieces):
        both = [y.reshape(D, 1, 8, W) for y in pieces]
        small_send[:, p] = jnp.concatenate(both, 1).reshape(D, 16, W).astype(bf16)

    def put_rows(ref, at, x):
        rows = ref.shape[1]
        x = x.astype(bf16)
        for k in range(x.shape[0] // 16):
            r = at + 16 * k
            ref[r // rows, r % rows : r % rows + 16] = x[16 * k : 16 * k + 16]

    def out_grad(u):
        return dot(xz_ref[u], dres_ref[u], 1, 1)

    def spread(x, row, step):
        a_ref[pl.ds(row, step)] = x[:, 0:C]
        a_ref[pl.ds(row + step, step)] = x[:, C : 2 * C]
        tail = x[:, 2 * C : W]
        b_ref[pl.ds(row, step)] = tail
        b_ref[pl.ds(row + step, step)] = pltpu.roll(tail, 64, 1)

    def collect(row, step):
        lane = lax.broadcasted_iota(jnp.int32, (step, C), 1)
        tail = jnp.where(lane < 64, b_ref[pl.ds(row, step)], b_ref[pl.ds(row + step, step)])
        return jnp.concatenate([a_ref[pl.ds(row, step)], a_ref[pl.ds(row + step, step)], tail], 1)

    def get_channel(ch, step):
        a = a_ref[pl.ds(ch, N, stride=step), :]
        b = b_ref[pl.ds(ch, N, stride=step), :]
        return a.astype(bf16), b[:, :64].astype(bf16)

    def put_channel(ch, step, x):
        a_ref[pl.ds(ch, N, stride=step), :] = x[:, 0:C]
        b_ref[pl.ds(ch, N, stride=step), :] = jnp.concatenate([x[:, C:N], x[:, C:N]], 1)

    def arrive(send, recv, phase, k):
        src = src_of(k)

        @pl.when(k == 0)
        def _():
            own_copy(send, recv, phase).wait()

        @pl.when(k > 0)
        def _():
            wait_from(send, recv, phase, src)

        return src

    def depart(send, recv, phase, k):
        peer = peer_of(k)

        @pl.when(k == 0)
        def _():
            own_copy(send, recv, phase).start()

        @pl.when(k > 0)
        def _():
            send_to(send, recv, phase, peer)

    def products(u, phase, slot):
        recv = big_recv.at[slot]

        @pl.loop(0, D)
        def _(k):
            src = arrive(big_send, recv, phase, k)
            for c in range(CH):
                spread(big_recv[slot, src, c].astype(f32), (src * R + 2 * c) * 16, 16)

        for ch in range(16):
            a, b = get_channel(ch, 16)
            lm_ref[u, ch, :, 0:C] = a
            lm_ref[u, ch, :, C:N] = b
        for ch in range(8):
            left, right = lm_ref[u, ch], lm_ref[u, 8 + ch]
            axis = 1 - u
            put_channel(ch, 8, dot(left, right, axis, axis))

        @pl.loop(0, D)
        def _(k):
            peer = peer_of(k)
            for p in range(CH // 2):
                row = (peer * R + 4 * p) * 8
                both = jnp.concatenate([collect(row, 8), collect(row + 16, 8)], 0)
                small_send[peer, p] = both.astype(bf16)
            depart(small_send, small_recv.at[slot], phase + 1, k)

    def product_grads(u, phase, slot):
        recv = small_recv.at[slot]

        @pl.loop(0, D)
        def _(k):
            src = arrive(small_send, recv, phase, k)
            for p in range(CH // 2):
                x = small_recv[slot, src, p].astype(f32)
                row = (src * R + 4 * p) * 8
                spread(x[0:8], row, 8)
                spread(x[8:16], row + 16, 8)

        for ch in range(8):
            a, b = get_channel(ch, 8)
            tm_ref[ch, :, 0:C] = a
            tm_ref[ch, :, C:N] = b
        for ch in range(8):
            left, right, grad = lm_ref[u, ch], lm_ref[u, 8 + ch], tm_ref[ch]
            if u == 0:
                dleft, dright = dot(grad, right, 1, 0), dot(grad, left, 0, 0)
            else:
                dleft, dright = dot(right, grad, 1, 1), dot(left, grad, 1, 0)
            put_channel(ch, 16, dleft)
            put_channel(8 + ch, 16, dright)

        @pl.loop(0, D)
        def _(k):
            peer = peer_of(k)
            for c in range(CH):
                big_send[peer, c] = collect((peer * R + 2 * c) * 16, 16).astype(bf16)
            depart(big_send, big_recv.at[slot], phase + 1, k)

    def start_sum(rows, arrived, phase):
        own_copy(rows, arrived, phase).start()

        @pl.loop(1, D)
        def _(k):
            send_to(rows, arrived, phase, peer_of(k))

    def mate_copy(src, dst, n):
        return pltpu.make_async_remote_copy(
            src_ref=src, dst_ref=dst, send_sem=core_s.at[n], recv_sem=core_r.at[n],
            device_id={"dp": mate}, device_id_type=MESH,
        )

    def z_copy(zbuf, n, peer, slot):
        return pltpu.make_async_remote_copy(
            src_ref=zbuf.at[slot], dst_ref=zbuf.at[slot],
            send_sem=zs.at[n, peer // 2], recv_sem=zr.at[n, slot],
            device_id={"dp": peer}, device_id_type=MESH,
        )

    def round_copy(everyone, phase, peer, slot):
        return pltpu.make_async_remote_copy(
            src_ref=everyone.at[slot], dst_ref=everyone.at[slot],
            send_sem=ssem.at[phase, peer], recv_sem=rsem.at[phase, slot],
            device_id={"dap": peer}, device_id_type=MESH,
        )

    def finish_sum(rows, arrived, phase, zbuf, everyone, n):
        half = rows.shape[1] // 2
        wait_all(rows, arrived, phase)

        def add(k, acc):
            return acc + arrived[k].astype(f32)

        total = lax.fori_loop(1, D, add, arrived[0].astype(f32))
        mine = jnp.where(core == 0, total[:half], total[half:])
        theirs = jnp.where(core == 0, total[half:], total[:half])
        half_out[n, 0:half] = theirs
        swap = mate_copy(half_out.at[n, pl.ds(0, half)], half_in.at[n, pl.ds(0, half)], n)
        swap.start()
        swap.wait_recv()
        zbuf[zed] = (mine + half_in[n, 0:half]).astype(bf16)

        @pl.loop(1, nz)
        def _(k):
            z_copy(zbuf, n, z_peer(k), zed).start()

        wait_sends(rows, arrived, phase)
        swap.wait_send()

        @pl.loop(1, nz)
        def _(k):
            peer = z_peer(nz - k)
            z_copy(zbuf, n, peer, peer // 2).wait_recv()

        def add_z(k, acc):
            return acc + zbuf[k].astype(f32)

        total = lax.fori_loop(1, nz, add_z, zbuf[0].astype(f32)).astype(bf16)
        mine = pl.ds(pl.multiple_of(core * half, half), half)
        everyone[me, mine] = total
        back = mate_copy(everyone.at[me, mine], everyone.at[me, mine], 2 + n)
        back.start()
        back.wait_recv()
        back.wait_send()

        @pl.loop(1, D)
        def _(k):
            round_copy(everyone, 10 + n, peer_of(k), me).start()

        @pl.loop(1, nz)
        def _(k):
            z_copy(zbuf, n, z_peer(k), zed).wait_send()

    def wait_round(everyone, phase):
        @pl.loop(1, D)
        def _(k):
            src = src_of(k)
            round_copy(everyone, phase, src, src).wait_recv()

        @pl.loop(1, D)
        def _(k):
            round_copy(everyone, phase, peer_of(k), me).wait_send()

    @pl.loop(0, CH)
    def _(c):
        project(0, c, load_cells(pair_ref, c))

    pl.semaphore_wait(barrier, D - 1 + nz)
    send_all(big_send, big_recv.at[0], 0)
    products(0, 0, 0)
    wait_sends(big_send, big_recv.at[0], 0)
    wait_all(small_send, small_recv.at[0], 1)

    @pl.loop(0, CH // 2)
    def _(p):
        for a, t in enumerate(halves(0, p)):
            c = 2 * p + a
            res = finish_product(0, c, t)
            one = (load_cells(pair_ref, c) + gate_ref[0, c] * res).astype(bf16)
            project(1, c, one.astype(f32))

    send_all(big_send, big_recv.at[1], 2)
    wait_sends(small_send, small_recv.at[0], 1)
    products(1, 2, 1)
    wait_sends(big_send, big_recv.at[1], 2)
    wait_all(small_send, small_recv.at[1], 3)
    wait_sends(small_send, small_recv.at[1], 3)

    @pl.loop(0, CH // 2)
    def _(p):
        pieces = []
        for a, t in enumerate(halves(1, p)):
            c = 2 * p + a
            finish_product(1, c, t)
            pieces.append(back_to_product(1, c, load_cells(cot_ref, c)))
        put_halves(p, pieces)

    send_all(small_send, small_recv.at[2], 4)
    put_rows(early, 5 * C, out_grad(1))
    product_grads(1, 4, 2)
    wait_sends(small_send, small_recv.at[2], 4)
    wait_all(big_send, big_recv.at[2], 5)

    @pl.loop(0, CH // 2)
    def _(p):
        pieces = []
        for a in range(2):
            c = 2 * p + a
            back_to_factors(1, c, 2)
            up = (load_cells(cot_ref, c) + back_to_pair(1, c)).astype(bf16)
            up_ref[c] = up
            pieces.append(back_to_product(0, c, up.astype(f32)))
        put_halves(p, pieces)

    send_all(small_send, small_recv.at[3], 6)
    wait_sends(big_send, big_recv.at[2], 5)
    put_rows(early, 0, dot(dq_ref[1], z_ref[1], 1, 1))
    put_rows(early, 6 * C, out_grad(0))
    put_rows(early, 7 * C, dot(dq_ref[0, 4 * C : 5 * C], z_ref[0], 1, 1))
    start_sum(early, early_in, 8)
    product_grads(0, 6, 3)
    wait_sends(small_send, small_recv.at[3], 6)
    finish_sum(early, early_in, 8, z_early, early_all, 0)
    wait_all(big_send, big_recv.at[3], 7)

    @pl.loop(0, CH)
    def _(c):
        back_to_factors(0, c, 3)

    put_rows(late, 0, dot(dq_ref[0, 0 : 4 * C], z_ref[0], 1, 1))
    start_sum(late, late_in, 9)

    @pl.loop(0, CH)
    def _(c):
        total = up_ref[c].astype(f32) + back_to_pair(0, c)
        y = jnp.transpose(total).astype(bf16)
        i = 2 * c
        out_ref[i, 0:C] = y[0:C]
        out_ref[i + 1, 0:C] = y[C : 2 * C]
        out_ref[i, C:N] = y[2 * C : 2 * C + 64]
        out_ref[i + 1, C:N] = y[2 * C + 64 : W]

    wait_sends(big_send, big_recv.at[3], 7)
    finish_sum(late, late_in, 9, z_late, late_all, 1)
    wait_round(early_all, 10)
    wait_round(late_all, 11)

    def factors(x):
        blocks = []
        for e in range(2):
            for t in range(2):
                part = x[t * 2 * C : (t + 1) * 2 * C].reshape(D, 2, 8, C)[:, e]
                blocks.append(jnp.transpose(part.reshape(C, C)))
        return blocks

    first = early_all[...].astype(f32).reshape(EARLY, C) * (1.0 / N)
    last = late_all[...].astype(f32).reshape(LATE, C) * (1.0 / N)
    for u, x, gate in ((0, last, first[7 * C : 8 * C]), (1, first[0 : 4 * C], first[4 * C : 5 * C])):
        for k, block in enumerate(factors(x) + [jnp.transpose(gate)]):
            gin_ref[u, :, k * C : (k + 1) * C] = block
    gout_ref[0] = first[6 * C : 7 * C]
    gout_ref[1] = first[5 * C : 6 * C]


def local(ndp, pair, pair_cot, residue_mask, w_in, w_out):
    vmem = pl.BlockSpec(memory_space=pltpu.VMEM)
    nz = ndp // 2
    scratch = [
        pltpu.VMEM((2, 5 * C, C), bf16),
        pltpu.VMEM((2, C, 5 * C), bf16),
        pltpu.VMEM((2, C, C), bf16),
        pltpu.VMEM((2, CH, C, W), f32),
        pltpu.VMEM((2, CH, 1, W), f32),
        pltpu.VMEM((2, C, CELLS), bf16),
        pltpu.VMEM((2, CH, 2 * C, W), f32),
        pltpu.VMEM((2, CH, 2 * C, W), f32),
        pltpu.VMEM((2, CH, C, W), f32),
        pltpu.VMEM((2, CH, C, W), f32),
        pltpu.VMEM((2, CH, C, W), f32),
        pltpu.VMEM((2, CH, 1, W), f32),
        pltpu.VMEM((2, C, CELLS), bf16),
        pltpu.VMEM((CH, C, W), bf16),
        pltpu.VMEM((2, C, CELLS), bf16),
        pltpu.VMEM((2, 5 * C, CELLS), bf16),
        pltpu.VMEM((2, 16, N, N), bf16),
        pltpu.VMEM((8, N, N), bf16),
        pltpu.VMEM((N * 16, C), f32),
        pltpu.VMEM((N * 16, C), f32),
        pltpu.VMEM((D, CH, 16, W), bf16),
        pltpu.VMEM((D, CH // 2, 16, W), bf16),
        pltpu.VMEM((4, D, CH, 16, W), bf16),
        pltpu.VMEM((4, D, CH // 2, 16, W), bf16),
        pltpu.VMEM((D, EARLY // D, C), bf16),
        pltpu.VMEM((D, LATE // D, C), bf16),
        pltpu.VMEM((D, EARLY // D, C), bf16),
        pltpu.VMEM((D, LATE // D, C), bf16),
        pltpu.VMEM((2, EARLY // D // 2, C), f32),
        pltpu.VMEM((2, EARLY // D // 2, C), f32),
        pltpu.VMEM((nz, EARLY // D // 2, C), bf16),
        pltpu.VMEM((nz, LATE // D // 2, C), bf16),
        pltpu.VMEM((D, EARLY // D, C), bf16),
        pltpu.VMEM((D, LATE // D, C), bf16),
        pltpu.SemaphoreType.DMA((12, D)),
        pltpu.SemaphoreType.DMA((12, D)),
        pltpu.SemaphoreType.DMA((12,)),
        pltpu.SemaphoreType.DMA((4,)),
        pltpu.SemaphoreType.DMA((4,)),
        pltpu.SemaphoreType.DMA((2, nz)),
        pltpu.SemaphoreType.DMA((2, nz)),
    ]
    grad, in_total, out_total = pl.pallas_call(
        functools.partial(kernel, ndp),
        out_shape=(
            jax.ShapeDtypeStruct((R, N, C), bf16),
            jax.ShapeDtypeStruct((2, C, 5 * C), f32),
            jax.ShapeDtypeStruct((2, C, C), f32),
        ),
        in_specs=[vmem] * 5,
        out_specs=(vmem, vmem, vmem),
        scratch_shapes=scratch,
        compiler_params=pltpu.CompilerParams(
            collective_id=0, has_side_effects=True, vmem_limit_bytes=60 * 1024 * 1024
        ),
    )(pair[0], pair_cot[0], residue_mask, w_in, w_out)
    return grad[None], in_total, out_total


def solution(mesh):
    return jax.shard_map(
        functools.partial(local, mesh.shape["dp"]),
        mesh=mesh,
        in_specs=(P("dp", "dap", None, None), P("dp", "dap", None, None), P("dp", None), P(), P()),
        out_specs=(P("dp", "dap", None, None), P(), P()),
        check_vma=False,
    )
```

```python
import functools

import jax
import jax.numpy as jnp
from jax import lax
from jax.experimental import pallas as pl
from jax.experimental.pallas import tpu as pltpu
from jax.sharding import PartitionSpec as P

EPS = 1e-05
D = 16
R = 12
N = 192
C = 128
CH = 6
W = 2 * N
CELLS = R * N
EARLY = 8 * C
LATE = 4 * C
FAR = (10, 6, 9, 11, 14, 2, 8, 5, 7, 13, 15, 1, 4, 3, 12)
f32 = jnp.float32
bf16 = jnp.bfloat16
MESH = pl.DeviceIdType.MESH


def dot(a, b, ca, cb):
    return lax.dot_general(a, b, (((ca,), (cb,)), ((), ())), preferred_element_type=f32)


def normal_form(x):
    centred = x - jnp.mean(x, 0, keepdims=True)
    inv = lax.rsqrt(jnp.mean(centred * centred, 0, keepdims=True) + EPS)
    return centred * inv, inv


def norm_back(d, n, inv):
    return inv * (d - jnp.mean(d, 0, keepdims=True) - n * jnp.mean(d * n, 0, keepdims=True))


def kernel(
    ndp,
    pair_ref, cot_ref, mask_ref, win_ref, wo_ref,
    out_ref, gin_ref, gout_ref,
    wt_ref, wp_ref, wot_ref,
    n_ref, inv_ref, z_ref, v_ref, sg_ref, gate_ref, res_ref, ntri_ref, itri_ref, xz_ref,
    up_ref, dres_ref, dq_ref, lm_ref, tm_ref, a_ref, b_ref,
    big_send, small_send, big_recv, small_recv,
    early, late, early_in, late_in, half_mine, half_out, half_in, z_early, z_late, early_all, late_all,
    ssem, rsem, lsem, core_s, core_r, zs, zr, stagger,
):
    me = lax.axis_index("dap")
    my = lax.axis_index("dp")
    core, zed, nz = lax.rem(my, 2), my // 2, ndp // 2
    mate = my + 1 - 2 * core

    def offset(k, sign):
        j = k * 0
        for n, step in enumerate(FAR):
            j = jnp.where(k == n + 1, step, j)
        a, b = j // 4, lax.rem(j, 4)
        dx, dy = a + core * (b - a), b + core * (a - b)
        return lax.rem(me // 4 + 4 + sign * dx, 4) * 4 + lax.rem(lax.rem(me, 4) + 4 + sign * dy, 4)

    def peer_of(k):
        return offset(k, 1)

    def src_of(k):
        return offset(k, -1)

    def z_peer(k):
        return 2 * lax.rem(zed + k, nz) + core

    barrier = pltpu.get_barrier_semaphore()

    @pl.loop(1, D)
    def _(k):
        pl.semaphore_signal(barrier, inc=1, device_id={"dap": peer_of(k)}, device_id_type=MESH)

    pl.semaphore_signal(barrier, inc=1, device_id={"dp": mate}, device_id_type=MESH)

    @pl.loop(1, nz)
    def _(k):
        pl.semaphore_signal(barrier, inc=1, device_id={"dp": z_peer(k)}, device_id_type=MESH)

    for u in range(2):
        wt = jnp.transpose(win_ref[u].astype(f32))
        pieces = []
        for t in range(2):
            left, right = (wt[(2 * e + t) * C : (2 * e + t + 1) * C].reshape(D, 8, C) for e in range(2))
            for g in range(2):
                at = slice(4 * g, 4 * g + 4)
                pieces.append(jnp.concatenate([left[:, at], right[:, at]], 1).reshape(C, C))
        wt = jnp.concatenate(pieces + [wt[4 * C : 5 * C]], 0)
        wt_ref[u] = wt.astype(bf16)
        wp_ref[u] = jnp.transpose(wt).astype(bf16)
        wot_ref[u] = jnp.transpose(wo_ref[u].astype(f32)).astype(bf16)

    count = jnp.sum(mask_ref[...].astype(f32), 1, keepdims=True)

    def cell_mask(c):
        lane = lax.broadcasted_iota(jnp.int32, (1, W), 1)
        second = ((lane >= C) & (lane < 2 * C)) | (lane >= 2 * C + 64)
        k = jnp.where(lane < C, lane, jnp.where(lane < 2 * C + 64, lane - C, lane - N))
        k = jnp.where((lane >= C) & (lane < 2 * C), lane - C, k)
        row = me * R + 2 * c + second.astype(jnp.int32)
        return jnp.where((jnp.maximum(k, row).astype(f32) < count), 1.0, 0.0).astype(f32)

    def cells(c):
        return pl.ds(pl.multiple_of(c * W, C), W)

    def load_cells(ref, c):
        i = 2 * c
        x = jnp.concatenate(
            [ref[i, 0:C], ref[i + 1, 0:C], ref[i, C:N], ref[i + 1, C:N]], 0
        )
        return jnp.transpose(x.astype(f32))

    def copy_of(send, recv, phase, peer, slot, src):
        return pltpu.make_async_remote_copy(
            src_ref=send.at[peer],
            dst_ref=recv.at[slot],
            send_sem=ssem.at[phase, peer],
            recv_sem=rsem.at[phase, src],
            device_id={"dap": peer},
            device_id_type=MESH,
        )

    def send_to(send, recv, phase, peer):
        copy_of(send, recv, phase, peer, me, me).start()

    def own_copy(send, recv, phase):
        return pltpu.make_async_copy(send.at[me], recv.at[me], lsem.at[phase])

    def wait_from(send, recv, phase, src):
        copy_of(send, recv, phase, src, src, src).wait_recv()

    def send_all(send, recv, phase):
        own_copy(send, recv, phase).start()

        @pl.loop(1, D)
        def _(k):
            send_to(send, recv, phase, peer_of(k))

    def wait_sends(send, recv, phase):
        @pl.loop(1, D)
        def _(k):
            copy_of(send, recv, phase, peer_of(k), me, me).wait_send()

    def wait_all(send, recv, phase):
        own_copy(send, recv, phase).wait()

        @pl.loop(1, D)
        def _(k):
            wait_from(send, recv, phase, src_of(k))

    def normalize(u, c, x):
        n, inv = normal_form(x)
        n_ref[u, c] = n
        inv_ref[u, c] = inv
        z_ref[u, :, cells(c)] = n.astype(bf16)

    def factors_of(u, c, g):
        z = z_ref[u, :, cells(c)]
        v = dot(wt_ref[u, g * C : (g + 1) * C], z, 1, 0)
        sg = jax.nn.sigmoid(dot(wt_ref[u, (2 + g) * C : (3 + g) * C], z, 1, 0))
        v_ref[u, c, g * C : (g + 1) * C] = v
        sg_ref[u, c, g * C : (g + 1) * C] = sg
        return sg * v * cell_mask(c)

    def second_group(u):
        @pl.loop(0, CH // 2)
        def _(p):
            put_halves(big_send.at[1], p, [factors_of(u, 2 * p + a, 1) for a in range(2)])
            for a in range(2):
                c = 2 * p + a
                gate_ref[u, c] = jax.nn.sigmoid(dot(wt_ref[u, 4 * C : 5 * C], z_ref[u, :, cells(c)], 1, 0))

    def finish_product(u, c, t):
        n, inv = normal_form(t)
        ntri_ref[u, c] = n
        itri_ref[u, c] = inv
        xz = n.astype(bf16)
        xz_ref[u, :, cells(c)] = xz
        res = dot(wot_ref[u], xz, 1, 0)
        res_ref[u, c] = res
        return res

    def back_to_product(u, c, up):
        gate = gate_ref[u, c]
        dres = (up * gate).astype(bf16)
        dres_ref[u, :, cells(c)] = dres
        dq_ref[u, 4 * C : 5 * C, cells(c)] = (up * res_ref[u, c] * gate * (1.0 - gate)).astype(bf16)
        return norm_back(dot(wo_ref[u], dres, 1, 0), ntri_ref[u, c], itri_ref[u, c])

    def back_to_factors(u, p, g, slot):
        for a, d in enumerate(halves(big_recv.at[slot, g], p)):
            c = 2 * p + a
            sg = sg_ref[u, c, g * C : (g + 1) * C]
            dv = d * sg * cell_mask(c)
            dq_ref[u, g * C : (g + 1) * C, cells(c)] = dv.astype(bf16)
            dg = dv * v_ref[u, c, g * C : (g + 1) * C] * (1.0 - sg)
            dq_ref[u, (2 + g) * C : (3 + g) * C, cells(c)] = dg.astype(bf16)

    def back_to_pair(u, c):
        d = dot(wp_ref[u], dq_ref[u, :, cells(c)], 1, 0)
        return norm_back(d, n_ref[u, c], inv_ref[u, c])

    def halves(ref, p):
        x = ref[:, p].astype(f32).reshape(D, 2, 8, W)
        return x[:, 0].reshape(C, W), x[:, 1].reshape(C, W)

    def put_halves(ref, p, pieces):
        both = [y.reshape(D, 1, 8, W) for y in pieces]
        ref[:, p] = jnp.concatenate(both, 1).reshape(D, 16, W).astype(bf16)

    def put_rows(ref, at, x):
        rows = ref.shape[1]
        x = x.astype(bf16)
        for k in range(x.shape[0] // 16):
            r = at + 16 * k
            ref[r // rows, r % rows : r % rows + 16] = x[16 * k : 16 * k + 16]

    def out_grad(u):
        return dot(xz_ref[u], dres_ref[u], 1, 1)

    def spread(q, x, row):
        a_ref[q, pl.ds(row, 8)] = x[:, 0:C]
        a_ref[q, pl.ds(row + 8, 8)] = x[:, C : 2 * C]
        tail = x[:, 2 * C : W]
        b_ref[q, pl.ds(row, 8)] = tail
        b_ref[q, pl.ds(row + 8, 8)] = pltpu.roll(tail, 64, 1)

    def collect(q, row):
        lane = lax.broadcasted_iota(jnp.int32, (8, C), 1)
        tail = jnp.where(lane < 64, b_ref[q, pl.ds(row, 8)], b_ref[q, pl.ds(row + 8, 8)])
        return jnp.concatenate([a_ref[q, pl.ds(row, 8)], a_ref[q, pl.ds(row + 8, 8)], tail], 1)

    def get_channel(q, ch):
        a = a_ref[q, pl.ds(ch, N, stride=8), :]
        b = b_ref[q, pl.ds(ch, N, stride=8), :]
        return a.astype(bf16), b[:, :64].astype(bf16)

    def put_channel(q, ch, x):
        a_ref[q, pl.ds(ch, N, stride=8), :] = x[:, 0:C]
        b_ref[q, pl.ds(ch, N, stride=8), :] = jnp.concatenate([x[:, C:N], x[:, C:N]], 1)

    def arrive(send, recv, phase, k):
        src = src_of(k)

        @pl.when(k == 0)
        def _():
            own_copy(send, recv, phase).wait()

        @pl.when(k > 0)
        def _():
            wait_from(send, recv, phase, src)

        return src

    def depart(send, recv, phase, k):
        peer = peer_of(k)

        @pl.when(k == 0)
        def _():
            own_copy(send, recv, phase).start()

        @pl.when(k > 0)
        def _():
            send_to(send, recv, phase, peer)

    def unpack(q, send, recv, phase):
        @pl.loop(0, D)
        def _(k):
            src = arrive(send, recv, phase, k)
            for p in range(CH // 2):
                x = recv[src, p].astype(f32)
                row = (src * R + 4 * p) * 8
                spread(q, x[0:8], row)
                spread(q, x[8:16], row + 16)

    def pack(q, send, recv, phase):
        @pl.loop(0, D)
        def _(k):
            peer = peer_of(k)
            for p in range(CH // 2):
                row = (peer * R + 4 * p) * 8
                send[peer, p] = jnp.concatenate([collect(q, row), collect(q, row + 16)], 0).astype(bf16)
            depart(send, recv, phase, k)

    def products(u, phase, slot):
        for g in range(2):
            unpack(g, big_send.at[g], big_recv.at[slot, g], phase + g)
            for ch in range(8):
                a, b = get_channel(g, ch)
                lm_ref[u, g, ch, :, 0:C] = a
                lm_ref[u, g, ch, :, C:N] = b
            for e in range(4):
                axis = 1 - u
                put_channel(2, 4 * g + e, dot(lm_ref[u, g, e], lm_ref[u, g, 4 + e], axis, axis))
        pack(2, small_send, small_recv.at[slot], phase + 2)

    def product_grads(u, phase, slot):
        unpack(2, small_send, small_recv.at[slot], phase)
        for ch in range(8):
            a, b = get_channel(2, ch)
            tm_ref[ch, :, 0:C] = a
            tm_ref[ch, :, C:N] = b
        for g in range(2):
            for e in range(4):
                left, right, grad = lm_ref[u, g, e], lm_ref[u, g, 4 + e], tm_ref[4 * g + e]
                if u == 0:
                    dleft, dright = dot(grad, right, 1, 0), dot(grad, left, 0, 0)
                else:
                    dleft, dright = dot(right, grad, 1, 1), dot(left, grad, 1, 0)
                put_channel(g, e, dleft)
                put_channel(g, 4 + e, dright)
            pack(g, big_send.at[g], big_recv.at[slot, g], phase + 1 + g)

    def start_sum(rows, arrived, phase):
        own_copy(rows, arrived, phase).start()

        @pl.loop(1, D)
        def _(k):
            send_to(rows, arrived, phase, peer_of(k))

    def mate_copy(src, dst, n):
        return pltpu.make_async_remote_copy(
            src_ref=src, dst_ref=dst, send_sem=core_s.at[n], recv_sem=core_r.at[n],
            device_id={"dp": mate}, device_id_type=MESH,
        )

    def z_copy(zbuf, n, peer, slot):
        return pltpu.make_async_remote_copy(
            src_ref=zbuf.at[slot], dst_ref=zbuf.at[slot],
            send_sem=zs.at[n, peer // 2], recv_sem=zr.at[n, slot],
            device_id={"dp": peer}, device_id_type=MESH,
        )

    def round_copy(everyone, phase, peer, slot):
        return pltpu.make_async_remote_copy(
            src_ref=everyone.at[slot], dst_ref=everyone.at[slot],
            send_sem=ssem.at[phase, peer], recv_sem=rsem.at[phase, slot],
            device_id={"dap": peer}, device_id_type=MESH,
        )

    def own_half(rows):
        half = rows.shape[1] // 2
        return pl.ds(pl.multiple_of(core * half, half), half)

    def swap_halves(rows, n):
        half = rows.shape[1] // 2
        return mate_copy(half_out.at[n, pl.ds(0, half)], half_in.at[n, pl.ds(0, half)], n)

    def sum_over_dap(rows, arrived, phase, n):
        half = rows.shape[1] // 2
        wait_all(rows, arrived, phase)

        def add(k, acc):
            return acc + arrived[k].astype(f32)

        total = lax.fori_loop(1, D, add, arrived[0].astype(f32))
        half_mine[n, 0:half] = jnp.where(core == 0, total[:half], total[half:])
        half_out[n, 0:half] = jnp.where(core == 0, total[half:], total[:half])
        swap_halves(rows, n).start()

    def send_along_z(rows, zbuf, n):
        half = rows.shape[1] // 2
        swap_halves(rows, n).wait_recv()
        zbuf[zed] = (half_mine[n, 0:half] + half_in[n, 0:half]).astype(bf16)

        @pl.loop(1, nz)
        def _(k):
            z_copy(zbuf, n, z_peer(k), zed).start()

    def hand_round(rows, zbuf, everyone, phase, n):
        @pl.loop(1, nz)
        def _(k):
            peer = z_peer(nz - k)
            z_copy(zbuf, n, peer, peer // 2).wait_recv()

        def add(k, acc):
            return acc + zbuf[k].astype(f32)

        total = lax.fori_loop(1, nz, add, zbuf[0].astype(f32)).astype(bf16)
        mine = own_half(rows)
        everyone[me, mine] = total
        back = mate_copy(everyone.at[me, mine], everyone.at[me, mine], 2 + n)
        back.start()
        back.wait_recv()

        @pl.loop(1, D)
        def _(k):
            round_copy(everyone, phase, peer_of(k), me).start()

    def end_sum(rows, arrived, phase, zbuf, everyone, n):
        wait_sends(rows, arrived, phase)
        swap_halves(rows, n).wait_send()
        mate_copy(everyone.at[me, own_half(rows)], everyone.at[me, own_half(rows)], 2 + n).wait_send()

        @pl.loop(1, nz)
        def _(k):
            z_copy(zbuf, n, z_peer(k), zed).wait_send()

    def wait_round(everyone, phase):
        @pl.loop(1, D)
        def _(k):
            src = src_of(k)
            round_copy(everyone, phase, src, src).wait_recv()

        @pl.loop(1, D)
        def _(k):
            round_copy(everyone, phase, peer_of(k), me).wait_send()

    def big(slot, g):
        return big_send.at[g], big_recv.at[slot, g]

    def small(slot):
        return small_send, small_recv.at[slot]

    @pl.loop(0, CH // 2)
    def _(p):
        pieces = []
        for a in range(2):
            c = 2 * p + a
            normalize(0, c, load_cells(pair_ref, c))
            pieces.append(factors_of(0, c, 0))
        put_halves(big_send.at[0], p, pieces)

    pl.semaphore_wait(barrier, D - 1 + nz)

    @pl.when(core == 1)
    def _():
        pl.semaphore_wait(stagger, 1)

    send_all(*big(0, 0), 0)
    second_group(0)
    send_all(*big(0, 1), 1)
    wait_sends(*big(0, 0), 0)
    wait_sends(*big(0, 1), 1)

    @pl.when(core == 0)
    def _():
        pl.semaphore_signal(stagger, inc=1, device_id={"dp": mate}, device_id_type=MESH)

    products(0, 0, 0)
    wait_all(*small(0), 2)

    @pl.loop(0, CH // 2)
    def _(p):
        pieces = []
        for a, t in enumerate(halves(small_recv.at[0], p)):
            c = 2 * p + a
            res = finish_product(0, c, t)
            one = (load_cells(pair_ref, c) + gate_ref[0, c] * res).astype(bf16)
            normalize(1, c, one.astype(f32))
            pieces.append(factors_of(1, c, 0))
        put_halves(big_send.at[0], p, pieces)

    send_all(*big(1, 0), 3)
    second_group(1)
    send_all(*big(1, 1), 4)
    wait_sends(*small(0), 2)
    products(1, 3, 1)
    wait_sends(*big(1, 0), 3)
    wait_sends(*big(1, 1), 4)
    wait_all(*small(1), 5)
    wait_sends(*small(1), 5)

    @pl.loop(0, CH // 2)
    def _(p):
        pieces = []
        for a, t in enumerate(halves(small_recv.at[1], p)):
            c = 2 * p + a
            finish_product(1, c, t)
            pieces.append(back_to_product(1, c, load_cells(cot_ref, c)))
        put_halves(small_send, p, pieces)

    send_all(*small(2), 6)
    put_rows(early, 5 * C, out_grad(1))
    product_grads(1, 6, 2)
    wait_sends(*small(2), 6)
    wait_all(*big(2, 0), 7)

    @pl.loop(0, CH // 2)
    def _(p):
        back_to_factors(1, p, 0, 2)

    wait_all(*big(2, 1), 8)

    @pl.loop(0, CH // 2)
    def _(p):
        back_to_factors(1, p, 1, 2)
        pieces = []
        for a in range(2):
            c = 2 * p + a
            up = (load_cells(cot_ref, c) + back_to_pair(1, c)).astype(bf16)
            up_ref[c] = up
            pieces.append(back_to_product(0, c, up.astype(f32)))
        put_halves(small_send, p, pieces)

    send_all(*small(3), 9)
    put_rows(early, 0, dot(dq_ref[1], z_ref[1], 1, 1))
    put_rows(early, 6 * C, out_grad(0))
    put_rows(early, 7 * C, dot(dq_ref[0, 4 * C : 5 * C], z_ref[0], 1, 1))
    start_sum(early, early_in, 12)
    wait_sends(*big(2, 0), 7)
    wait_sends(*big(2, 1), 8)
    product_grads(0, 9, 3)
    wait_sends(*small(3), 9)
    sum_over_dap(early, early_in, 12, 0)
    wait_all(*big(3, 0), 10)

    @pl.loop(0, CH // 2)
    def _(p):
        back_to_factors(0, p, 0, 3)

    send_along_z(early, z_early, 0)
    wait_all(*big(3, 1), 11)

    @pl.loop(0, CH // 2)
    def _(p):
        back_to_factors(0, p, 1, 3)

    put_rows(late, 0, dot(dq_ref[0, 0 : 4 * C], z_ref[0], 1, 1))
    start_sum(late, late_in, 13)

    @pl.loop(0, CH)
    def _(c):
        total = up_ref[c].astype(f32) + back_to_pair(0, c)
        y = jnp.transpose(total).astype(bf16)
        i = 2 * c
        out_ref[i, 0:C] = y[0:C]
        out_ref[i + 1, 0:C] = y[C : 2 * C]
        out_ref[i, C:N] = y[2 * C : 2 * C + 64]
        out_ref[i + 1, C:N] = y[2 * C + 64 : W]

    wait_sends(*big(3, 0), 10)
    wait_sends(*big(3, 1), 11)
    sum_over_dap(late, late_in, 13, 1)
    send_along_z(late, z_late, 1)
    hand_round(early, z_early, early_all, 14, 0)
    hand_round(late, z_late, late_all, 15, 1)
    wait_round(early_all, 14)
    wait_round(late_all, 15)
    end_sum(early, early_in, 12, z_early, early_all, 0)
    end_sum(late, late_in, 13, z_late, late_all, 1)

    def factors(x):
        blocks = []
        for e in range(2):
            for t in range(2):
                groups = [x[(2 * t + g) * C : (2 * t + g + 1) * C].reshape(D, 8, C) for g in range(2)]
                part = jnp.concatenate([y[:, 4 * e : 4 * e + 4] for y in groups], 1)
                blocks.append(jnp.transpose(part.reshape(C, C)))
        return blocks

    first = early_all[...].astype(f32).reshape(EARLY, C) * (1.0 / N)
    last = late_all[...].astype(f32).reshape(LATE, C) * (1.0 / N)
    for u, x, gate in ((0, last, first[7 * C : 8 * C]), (1, first[0 : 4 * C], first[4 * C : 5 * C])):
        for k, block in enumerate(factors(x) + [jnp.transpose(gate)]):
            gin_ref[u, :, k * C : (k + 1) * C] = block
    gout_ref[0] = first[6 * C : 7 * C]
    gout_ref[1] = first[5 * C : 6 * C]


def hand_over(a, b, c, x, y, z, sems):
    copies = [pltpu.make_async_copy(s, t, sems.at[k]) for k, (s, t) in enumerate(((a, x), (b, y), (c, z)))]
    for copy in copies:
        copy.start()
    for copy in copies:
        copy.wait()


def local(ndp, pair, pair_cot, residue_mask, w_in, w_out):
    vmem = pl.BlockSpec(memory_space=pltpu.VMEM)
    nz = ndp // 2
    scratch = [
        pltpu.VMEM((2, 5 * C, C), bf16),
        pltpu.VMEM((2, C, 5 * C), bf16),
        pltpu.VMEM((2, C, C), bf16),
        pltpu.VMEM((2, CH, C, W), f32),
        pltpu.VMEM((2, CH, 1, W), f32),
        pltpu.VMEM((2, C, CELLS), bf16),
        pltpu.VMEM((2, CH, 2 * C, W), f32),
        pltpu.VMEM((2, CH, 2 * C, W), f32),
        pltpu.VMEM((2, CH, C, W), f32),
        pltpu.VMEM((2, CH, C, W), f32),
        pltpu.VMEM((2, CH, C, W), f32),
        pltpu.VMEM((2, CH, 1, W), f32),
        pltpu.VMEM((2, C, CELLS), bf16),
        pltpu.VMEM((CH, C, W), bf16),
        pltpu.VMEM((2, C, CELLS), bf16),
        pltpu.VMEM((2, 5 * C, CELLS), bf16),
        pltpu.VMEM((2, 2, 8, N, N), bf16),
        pltpu.VMEM((8, N, N), bf16),
        pltpu.VMEM((3, N * 8, C), f32),
        pltpu.VMEM((3, N * 8, C), f32),
        pltpu.VMEM((2, D, CH // 2, 16, W), bf16),
        pltpu.VMEM((D, CH // 2, 16, W), bf16),
        pltpu.VMEM((4, 2, D, CH // 2, 16, W), bf16),
        pltpu.VMEM((4, D, CH // 2, 16, W), bf16),
        pltpu.VMEM((D, EARLY // D, C), bf16),
        pltpu.VMEM((D, LATE // D, C), bf16),
        pltpu.VMEM((D, EARLY // D, C), bf16),
        pltpu.VMEM((D, LATE // D, C), bf16),
        pltpu.VMEM((2, EARLY // D // 2, C), f32),
        pltpu.VMEM((2, EARLY // D // 2, C), f32),
        pltpu.VMEM((2, EARLY // D // 2, C), f32),
        pltpu.VMEM((nz, EARLY // D // 2, C), bf16),
        pltpu.VMEM((nz, LATE // D // 2, C), bf16),
        pltpu.VMEM((D, EARLY // D, C), bf16),
        pltpu.VMEM((D, LATE // D, C), bf16),
        pltpu.SemaphoreType.DMA((16, D)),
        pltpu.SemaphoreType.DMA((16, D)),
        pltpu.SemaphoreType.DMA((16,)),
        pltpu.SemaphoreType.DMA((4,)),
        pltpu.SemaphoreType.DMA((4,)),
        pltpu.SemaphoreType.DMA((2, nz)),
        pltpu.SemaphoreType.DMA((2, nz)),
        pltpu.SemaphoreType.REGULAR,
    ]
    grad, in_total, out_total = pl.pallas_call(
        functools.partial(kernel, ndp),
        out_shape=(
            jax.ShapeDtypeStruct((R, N, C), bf16),
            jax.ShapeDtypeStruct((2, C, 5 * C), f32),
            jax.ShapeDtypeStruct((2, C, C), f32),
        ),
        in_specs=[vmem] * 5,
        out_specs=(vmem, vmem, vmem),
        scratch_shapes=scratch,
        compiler_params=pltpu.CompilerParams(
            collective_id=0, has_side_effects=True, vmem_limit_bytes=60 * 1024 * 1024
        ),
    )(pair[0], pair_cot[0], residue_mask, w_in, w_out)
    results = (grad, in_total, out_total)
    anywhere = pl.BlockSpec(memory_space=pltpu.HBM)
    grad, in_total, out_total = pl.pallas_call(
        hand_over,
        out_shape=tuple(jax.ShapeDtypeStruct(x.shape, x.dtype) for x in results),
        in_specs=[vmem] * 3,
        out_specs=(anywhere,) * 3,
        scratch_shapes=[pltpu.SemaphoreType.DMA((3,))],
    )(*results)
    return grad[None], in_total, out_total


def solution(mesh):
    return jax.shard_map(
        functools.partial(local, mesh.shape["dp"]),
        mesh=mesh,
        in_specs=(P("dp", "dap", None, None), P("dp", "dap", None, None), P("dp", None), P(), P()),
        out_specs=(P("dp", "dap", None, None), P(), P()),
        check_vma=False,
    )
```

```python
import functools

import jax
import jax.numpy as jnp
from jax import lax
from jax.experimental import pallas as pl
from jax.experimental.pallas import tpu as pltpu
from jax.sharding import PartitionSpec as P

EPS = 1e-05
D = 16
R = 12
N = 192
C = 128
CH = 6
W = 2 * N
CELLS = R * N
EARLY = 8 * C
LATE = 4 * C
FAR = (10, 6, 9, 11, 14, 2, 8, 5, 7, 13, 15, 1, 4, 3, 12)
f32 = jnp.float32
bf16 = jnp.bfloat16
MESH = pl.DeviceIdType.MESH


def dot(a, b, ca, cb):
    return lax.dot_general(a, b, (((ca,), (cb,)), ((), ())), preferred_element_type=f32)


def sigmoid(x):
    return 0.5 * jnp.tanh(0.5 * x) + 0.5


def normal_form(x):
    centred = x - jnp.mean(x, 0, keepdims=True)
    inv = lax.rsqrt(jnp.mean(centred * centred, 0, keepdims=True) + EPS)
    return centred * inv, inv


def norm_back(d, n, inv):
    return inv * (d - jnp.mean(d, 0, keepdims=True) - n * jnp.mean(d * n, 0, keepdims=True))


def kernel(
    ndp,
    pair_ref, cot_ref, mask_ref, win_ref, wo_ref,
    out_ref, gin_ref, gout_ref,
    wt_ref, wp_ref, wot_ref,
    n_ref, inv_ref, z_ref, v_ref, sg_ref, gate_ref, res_ref, ntri_ref, itri_ref, xz_ref,
    pt_ref, ct_ref, up_ref, dres_ref, dq_ref, lm_ref, tm_ref, a_ref, b_ref,
    big_send, small_send, big_recv, small_recv,
    early, late, early_in, late_in, half_mine, half_out, half_in, z_early, z_late, early_all, late_all,
    ssem, rsem, lsem, gs, gr, own, core_s, core_r, zs, zr,
):
    me = lax.axis_index("dap")
    my = lax.axis_index("dp")
    core, zed, nz = lax.rem(my, 2), my // 2, ndp // 2
    mate = my + 1 - 2 * core

    def offset(k, sign):
        j = k * 0
        for n, step in enumerate(FAR):
            j = jnp.where(k == n + 1, step, j)
        a, b = j // 4, lax.rem(j, 4)
        dx, dy = a + core * (b - a), b + core * (a - b)
        return lax.rem(me // 4 + 4 + sign * dx, 4) * 4 + lax.rem(lax.rem(me, 4) + 4 + sign * dy, 4)

    def peer_of(k):
        return offset(k, 1)

    def src_of(k):
        return offset(k, -1)

    def z_peer(k):
        return 2 * lax.rem(zed + k, nz) + core

    barrier = pltpu.get_barrier_semaphore()

    @pl.loop(1, D)
    def _(k):
        pl.semaphore_signal(barrier, inc=1, device_id={"dap": peer_of(k)}, device_id_type=MESH)

    pl.semaphore_signal(barrier, inc=1, device_id={"dp": mate}, device_id_type=MESH)

    @pl.loop(1, nz)
    def _(k):
        pl.semaphore_signal(barrier, inc=1, device_id={"dp": z_peer(k)}, device_id_type=MESH)

    for u in range(2):
        wt = jnp.transpose(win_ref[u].astype(f32))
        pieces = []
        for t in range(2):
            left, right = (wt[(2 * e + t) * C : (2 * e + t + 1) * C].reshape(D, 8, C) for e in range(2))
            for g in range(2):
                at = slice(4 * g, 4 * g + 4)
                pieces.append(jnp.concatenate([left[:, at], right[:, at]], 1).reshape(C, C))
        wt = jnp.concatenate(pieces + [wt[4 * C : 5 * C]], 0)
        wt_ref[u] = wt.astype(bf16)
        wp_ref[u] = jnp.transpose(wt).astype(bf16)
        wot_ref[u] = jnp.transpose(wo_ref[u].astype(f32)).astype(bf16)

    count = jnp.sum(mask_ref[...].astype(f32), 1, keepdims=True)

    def cell_mask(c):
        lane = lax.broadcasted_iota(jnp.int32, (1, W), 1)
        second = ((lane >= C) & (lane < 2 * C)) | (lane >= 2 * C + 64)
        k = jnp.where(lane < C, lane, jnp.where(lane < 2 * C + 64, lane - C, lane - N))
        k = jnp.where((lane >= C) & (lane < 2 * C), lane - C, k)
        row = me * R + 2 * c + second.astype(jnp.int32)
        return jnp.where((jnp.maximum(k, row).astype(f32) < count), 1.0, 0.0).astype(f32)

    def cells(c):
        return pl.ds(pl.multiple_of(c * W, C), W)

    def load_cells(ref, c):
        i = 2 * c
        x = jnp.concatenate(
            [ref[i, 0:C], ref[i + 1, 0:C], ref[i, C:N], ref[i + 1, C:N]], 0
        )
        return jnp.transpose(x.astype(f32))

    def part_copy(send, recv, phase, p, peer, slot):
        return pltpu.make_async_remote_copy(
            src_ref=send.at[p, peer], dst_ref=recv.at[p, slot],
            send_sem=ssem.at[phase, p], recv_sem=rsem.at[phase, p],
            device_id={"dap": peer}, device_id_type=MESH,
        )

    def own_copy(send, recv, phase, p):
        return pltpu.make_async_copy(send.at[p, me], recv.at[p, me], lsem.at[phase, p])

    def others(send, recv, phase, p):
        rest = pl.ds(0, D - 1)
        return pltpu.make_async_remote_copy(
            src_ref=send.at[p, rest], dst_ref=recv.at[p, rest],
            send_sem=ssem.at[phase, p], recv_sem=rsem.at[phase, p],
            device_id={"dap": peer_of(1)}, device_id_type=MESH,
        )

    def send_part(send, recv, phase, p):
        own_copy(send, recv, phase, p).start()

        @pl.loop(1, D)
        def _(k):
            part_copy(send, recv, phase, p, peer_of(k), me).start()

    def wait_part(send, recv, phase, p):
        own_copy(send, recv, phase, p).wait()
        others(send, recv, phase, p).wait_recv()

    def wait_sends(send, recv, phase):
        for p in range(CH // 2):
            others(send, recv, phase, p).wait_send()

    def normalize(u, c, x):
        n, inv = normal_form(x)
        n_ref[u, c] = n
        inv_ref[u, c] = inv
        z_ref[u, :, cells(c)] = n.astype(bf16)

    def factors_of(u, c, g):
        z = z_ref[u, :, cells(c)]
        v = dot(wt_ref[u, g * C : (g + 1) * C], z, 1, 0)
        sg = sigmoid(dot(wt_ref[u, (2 + g) * C : (3 + g) * C], z, 1, 0))
        v_ref[u, c, g * C : (g + 1) * C] = v
        sg_ref[u, c, g * C : (g + 1) * C] = sg
        return sg * v * cell_mask(c)

    def second_group(u, send, recv, phase):
        @pl.loop(0, CH // 2)
        def _(p):
            put_halves(send, p, [factors_of(u, 2 * p + a, 1) for a in range(2)])
            send_part(send, recv, phase, p)
            for a in range(2):
                c = 2 * p + a
                gate_ref[u, c] = sigmoid(dot(wt_ref[u, 4 * C : 5 * C], z_ref[u, :, cells(c)], 1, 0))

    def finish_product(u, c, t):
        n, inv = normal_form(t)
        ntri_ref[u, c] = n
        itri_ref[u, c] = inv
        xz = n.astype(bf16)
        xz_ref[u, :, cells(c)] = xz
        res = dot(wot_ref[u], xz, 1, 0)
        res_ref[u, c] = res
        return res

    def back_to_product(u, c, up):
        gate = gate_ref[u, c]
        dres = (up * gate).astype(bf16)
        dres_ref[u, :, cells(c)] = dres
        dq_ref[u, 4 * C : 5 * C, cells(c)] = (up * res_ref[u, c] * gate * (1.0 - gate)).astype(bf16)
        return norm_back(dot(wo_ref[u], dres, 1, 0), ntri_ref[u, c], itri_ref[u, c])

    def back_to_factors(u, p, g, slot):
        for a, d in enumerate(halves(big_recv.at[slot, g], p)):
            c = 2 * p + a
            sg = sg_ref[u, c, g * C : (g + 1) * C]
            dv = d * sg * cell_mask(c)
            dq_ref[u, g * C : (g + 1) * C, cells(c)] = dv.astype(bf16)
            dg = dv * v_ref[u, c, g * C : (g + 1) * C] * (1.0 - sg)
            dq_ref[u, (2 + g) * C : (3 + g) * C, cells(c)] = dg.astype(bf16)

    def back_to_pair(u, c):
        d = dot(wp_ref[u], dq_ref[u, :, cells(c)], 1, 0)
        return norm_back(d, n_ref[u, c], inv_ref[u, c])

    def halves(ref, p):
        x = ref[p].astype(f32).reshape(D, 2, 8, W)
        return x[:, 0].reshape(C, W), x[:, 1].reshape(C, W)

    def put_halves(ref, p, pieces):
        both = [y.reshape(D, 1, 8, W) for y in pieces]
        ref[p] = jnp.concatenate(both, 1).reshape(D, 16, W).astype(bf16)

    def put_rows(ref, at, x):
        rows = ref.shape[1]
        x = x.astype(bf16)
        for k in range(x.shape[0] // 16):
            r = at + 16 * k
            ref[r // rows, r % rows : r % rows + 16] = x[16 * k : 16 * k + 16]

    def out_grad(u):
        return dot(xz_ref[u], dres_ref[u], 1, 1)

    def spread(q, x, row):
        a_ref[q, pl.ds(row, 8)] = x[:, 0:C]
        a_ref[q, pl.ds(row + 8, 8)] = x[:, C : 2 * C]
        tail = x[:, 2 * C : W]
        b_ref[q, pl.ds(row, 8)] = tail
        b_ref[q, pl.ds(row + 8, 8)] = pltpu.roll(tail, 64, 1)

    def collect(q, row):
        lane = lax.broadcasted_iota(jnp.int32, (8, C), 1)
        tail = jnp.where(lane < 64, b_ref[q, pl.ds(row, 8)], b_ref[q, pl.ds(row + 8, 8)])
        return jnp.concatenate([a_ref[q, pl.ds(row, 8)], a_ref[q, pl.ds(row + 8, 8)], tail], 1)

    def get_channel(q, ch):
        a = a_ref[q, pl.ds(ch, N, stride=8), :]
        b = b_ref[q, pl.ds(ch, N, stride=8), :]
        return a.astype(bf16), b[:, :64].astype(bf16)

    def put_channel(q, ch, x):
        a_ref[q, pl.ds(ch, N, stride=8), :] = x[:, 0:C]
        b_ref[q, pl.ds(ch, N, stride=8), :] = jnp.concatenate([x[:, C:N], x[:, C:N]], 1)

    def unpack(q, send, recv, phase):
        for p in range(CH // 2):
            wait_part(send, recv, phase, p)

            @pl.loop(0, D)
            def _(k):
                x = recv[p, k].astype(f32)
                row = (k * R + 4 * p) * 8
                spread(q, x[0:8], row)
                spread(q, x[8:16], row + 16)

    def pack(q, send, recv, phase):
        @pl.loop(0, CH // 2)
        def _(p):
            @pl.loop(0, D)
            def _(k):
                row = (k * R + 4 * p) * 8
                send[p, k] = jnp.concatenate([collect(q, row), collect(q, row + 16)], 0).astype(bf16)

            send_part(send, recv, phase, p)

    def products(u, phase, slot):
        for g in range(2):
            unpack(g, big_send.at[g], big_recv.at[slot, g], phase + g)
            for ch in range(8):
                a, b = get_channel(g, ch)
                lm_ref[u, g, ch, :, 0:C] = a
                lm_ref[u, g, ch, :, C:N] = b
            for e in range(4):
                axis = 1 - u
                put_channel(2, 4 * g + e, dot(lm_ref[u, g, e], lm_ref[u, g, 4 + e], axis, axis))
        pack(2, small_send, small_recv.at[slot], phase + 2)

    def product_grads(u, phase, slot):
        unpack(2, small_send, small_recv.at[slot], phase)
        for ch in range(8):
            a, b = get_channel(2, ch)
            tm_ref[ch, :, 0:C] = a
            tm_ref[ch, :, C:N] = b
        for g in range(2):
            for e in range(4):
                left, right, grad = lm_ref[u, g, e], lm_ref[u, g, 4 + e], tm_ref[4 * g + e]
                if u == 0:
                    dleft, dright = dot(grad, right, 1, 0), dot(grad, left, 0, 0)
                else:
                    dleft, dright = dot(right, grad, 1, 1), dot(left, grad, 1, 0)
                put_channel(g, e, dleft)
                put_channel(g, 4 + e, dright)
            pack(g, big_send.at[g], big_recv.at[slot, g], phase + 1 + g)

    def sum_copy(rows, arrived, n, peer, slot, dev=None):
        return pltpu.make_async_remote_copy(
            src_ref=rows.at[peer], dst_ref=arrived.at[slot], send_sem=gs.at[n], recv_sem=gr.at[n],
            device_id={"dap": peer if dev is None else dev}, device_id_type=MESH,
        )

    def own_rows(rows, arrived, n):
        return pltpu.make_async_copy(rows.at[me], arrived.at[me], own.at[n])

    def start_sum(rows, arrived, n):
        own_rows(rows, arrived, n).start()

        @pl.loop(1, D)
        def _(k):
            sum_copy(rows, arrived, n, peer_of(k), me).start()

    def mate_copy(src, dst, n):
        return pltpu.make_async_remote_copy(
            src_ref=src, dst_ref=dst, send_sem=core_s.at[n], recv_sem=core_r.at[n],
            device_id={"dp": mate}, device_id_type=MESH,
        )

    def z_copy(zbuf, n, peer, slot):
        return pltpu.make_async_remote_copy(
            src_ref=zbuf.at[slot], dst_ref=zbuf.at[slot],
            send_sem=zs.at[n], recv_sem=zr.at[n],
            device_id={"dp": peer}, device_id_type=MESH,
        )

    def round_copy(everyone, n, peer, slot):
        return pltpu.make_async_remote_copy(
            src_ref=everyone.at[slot], dst_ref=everyone.at[slot],
            send_sem=gs.at[2 + n], recv_sem=gr.at[2 + n],
            device_id={"dap": peer}, device_id_type=MESH,
        )

    rest = pl.ds(0, D - 1)
    rest_z = pl.ds(0, nz - 1)

    def own_half(rows):
        half = rows.shape[1] // 2
        return pl.ds(pl.multiple_of(core * half, half), half)

    def swap_halves(rows, n):
        half = rows.shape[1] // 2
        return mate_copy(half_out.at[n, pl.ds(0, half)], half_in.at[n, pl.ds(0, half)], n)

    def sum_over_dap(rows, arrived, n):
        half = rows.shape[1] // 2
        own_rows(rows, arrived, n).wait()
        sum_copy(rows, arrived, n, rest, rest, peer_of(1)).wait_recv()

        def add(k, acc):
            return acc + arrived[k].astype(f32)

        total = lax.fori_loop(1, D, add, arrived[0].astype(f32))
        half_mine[n, 0:half] = jnp.where(core == 0, total[:half], total[half:])
        half_out[n, 0:half] = jnp.where(core == 0, total[half:], total[:half])
        swap_halves(rows, n).start()

    def send_along_z(rows, zbuf, n):
        half = rows.shape[1] // 2
        swap_halves(rows, n).wait_recv()
        zbuf[zed] = (half_mine[n, 0:half] + half_in[n, 0:half]).astype(bf16)

        @pl.loop(1, nz)
        def _(k):
            z_copy(zbuf, n, z_peer(k), zed).start()

    def hand_round(rows, zbuf, everyone, n):
        if nz > 1:
            z_copy(zbuf, n, z_peer(1), rest_z).wait_recv()

        def add(k, acc):
            return acc + zbuf[k].astype(f32)

        total = lax.fori_loop(1, nz, add, zbuf[0].astype(f32)).astype(bf16)
        mine = own_half(rows)
        everyone[me, mine] = total
        back = mate_copy(everyone.at[me, mine], everyone.at[me, mine], 2 + n)
        back.start()
        back.wait_recv()

        @pl.loop(1, D)
        def _(k):
            round_copy(everyone, n, peer_of(k), me).start()

    def end_sum(rows, arrived, zbuf, everyone, n):
        sum_copy(rows, arrived, n, rest, rest, peer_of(1)).wait_send()
        round_copy(everyone, n, peer_of(1), rest).wait_send()
        swap_halves(rows, n).wait_send()
        mate_copy(everyone.at[me, own_half(rows)], everyone.at[me, own_half(rows)], 2 + n).wait_send()
        if nz > 1:
            z_copy(zbuf, n, z_peer(1), rest_z).wait_send()

    def big(slot, g):
        return big_send.at[g], big_recv.at[slot, g]

    def small(slot):
        return small_send, small_recv.at[slot]

    for p in range(CH // 2):
        pieces = []
        for a in range(2):
            c = 2 * p + a
            x = load_cells(pair_ref, c)
            pt_ref[c] = x.astype(bf16)
            normalize(0, c, x)
            pieces.append(factors_of(0, c, 0))
        put_halves(big_send.at[0], p, pieces)
        if p == 0:
            pl.semaphore_wait(barrier, D - 1 + nz)
        send_part(*big(0, 0), 0, p)
    second_group(0, *big(0, 1), 1)
    products(0, 0, 0)
    wait_sends(*big(0, 0), 0)
    wait_sends(*big(0, 1), 1)

    @pl.loop(0, CH // 2)
    def _(p):
        wait_part(*small(0), 2, p)
        pieces = []
        for a, t in enumerate(halves(small_recv.at[0], p)):
            c = 2 * p + a
            res = finish_product(0, c, t)
            one = (pt_ref[c].astype(f32) + gate_ref[0, c] * res).astype(bf16)
            normalize(1, c, one.astype(f32))
            pieces.append(factors_of(1, c, 0))
        put_halves(big_send.at[0], p, pieces)
        send_part(*big(1, 0), 3, p)

    second_group(1, *big(1, 1), 4)
    wait_sends(*small(0), 2)

    @pl.loop(0, CH)
    def _(c):
        ct_ref[c] = load_cells(cot_ref, c).astype(bf16)

    products(1, 3, 1)
    wait_sends(*big(1, 0), 3)
    wait_sends(*big(1, 1), 4)
    wait_sends(*small(1), 5)

    @pl.loop(0, CH // 2)
    def _(p):
        wait_part(*small(1), 5, p)
        pieces = []
        for a, t in enumerate(halves(small_recv.at[1], p)):
            c = 2 * p + a
            finish_product(1, c, t)
            pieces.append(back_to_product(1, c, ct_ref[c].astype(f32)))
        put_halves(small_send, p, pieces)
        send_part(*small(2), 6, p)

    put_rows(early, 5 * C, out_grad(1))
    product_grads(1, 6, 2)
    wait_sends(*small(2), 6)

    @pl.loop(0, CH // 2)
    def _(p):
        wait_part(*big(2, 0), 7, p)
        back_to_factors(1, p, 0, 2)

    @pl.loop(0, CH // 2)
    def _(p):
        wait_part(*big(2, 1), 8, p)
        back_to_factors(1, p, 1, 2)
        pieces = []
        for a in range(2):
            c = 2 * p + a
            up = (ct_ref[c].astype(f32) + back_to_pair(1, c)).astype(bf16)
            up_ref[c] = up
            pieces.append(back_to_product(0, c, up.astype(f32)))
        put_halves(small_send, p, pieces)
        send_part(*small(3), 9, p)

    put_rows(early, 0, dot(dq_ref[1], z_ref[1], 1, 1))
    put_rows(early, 6 * C, out_grad(0))
    put_rows(early, 7 * C, dot(dq_ref[0, 4 * C : 5 * C], z_ref[0], 1, 1))
    start_sum(early, early_in, 0)
    wait_sends(*big(2, 0), 7)
    wait_sends(*big(2, 1), 8)
    product_grads(0, 9, 3)
    wait_sends(*small(3), 9)
    sum_over_dap(early, early_in, 0)

    @pl.loop(0, CH // 2)
    def _(p):
        wait_part(*big(3, 0), 10, p)
        back_to_factors(0, p, 0, 3)

    send_along_z(early, z_early, 0)

    @pl.loop(0, CH // 2)
    def _(p):
        wait_part(*big(3, 1), 11, p)
        back_to_factors(0, p, 1, 3)

    put_rows(late, 0, dot(dq_ref[0, 0 : 4 * C], z_ref[0], 1, 1))
    start_sum(late, late_in, 1)

    @pl.loop(0, CH)
    def _(c):
        total = up_ref[c].astype(f32) + back_to_pair(0, c)
        y = jnp.transpose(total).astype(bf16)
        i = 2 * c
        out_ref[i, 0:C] = y[0:C]
        out_ref[i + 1, 0:C] = y[C : 2 * C]
        out_ref[i, C:N] = y[2 * C : 2 * C + 64]
        out_ref[i + 1, C:N] = y[2 * C + 64 : W]

    wait_sends(*big(3, 0), 10)
    wait_sends(*big(3, 1), 11)
    sum_over_dap(late, late_in, 1)
    send_along_z(late, z_late, 1)
    hand_round(early, z_early, early_all, 0)
    hand_round(late, z_late, late_all, 1)

    def factors(x):
        blocks = []
        for e in range(2):
            for t in range(2):
                groups = [x[(2 * t + g) * C : (2 * t + g + 1) * C].reshape(D, 8, C) for g in range(2)]
                part = jnp.concatenate([y[:, 4 * e : 4 * e + 4] for y in groups], 1)
                blocks.append(jnp.transpose(part.reshape(C, C)))
        return blocks

    round_copy(early_all, 0, peer_of(1), rest).wait_recv()
    first = early_all[...].astype(f32).reshape(EARLY, C) * (1.0 / N)
    for k, block in enumerate(factors(first[0 : 4 * C]) + [jnp.transpose(first[4 * C : 5 * C])]):
        gin_ref[1, :, k * C : (k + 1) * C] = block
    gin_ref[0, :, 4 * C : 5 * C] = jnp.transpose(first[7 * C : 8 * C])
    gout_ref[0] = first[6 * C : 7 * C]
    gout_ref[1] = first[5 * C : 6 * C]

    round_copy(late_all, 1, peer_of(1), rest).wait_recv()
    last = late_all[...].astype(f32).reshape(LATE, C) * (1.0 / N)
    for k, block in enumerate(factors(last)):
        gin_ref[0, :, k * C : (k + 1) * C] = block

    end_sum(early, early_in, z_early, early_all, 0)
    end_sum(late, late_in, z_late, late_all, 1)


def hand_over(a, b, c, x, y, z, sems):
    copies = [pltpu.make_async_copy(s, t, sems.at[k]) for k, (s, t) in enumerate(((a, x), (b, y), (c, z)))]
    for copy in copies:
        copy.start()
    for copy in copies:
        copy.wait()


def local(ndp, pair, pair_cot, residue_mask, w_in, w_out):
    vmem = pl.BlockSpec(memory_space=pltpu.VMEM)
    nz = ndp // 2
    scratch = [
        pltpu.VMEM((2, 5 * C, C), bf16),
        pltpu.VMEM((2, C, 5 * C), bf16),
        pltpu.VMEM((2, C, C), bf16),
        pltpu.VMEM((2, CH, C, W), f32),
        pltpu.VMEM((2, CH, 1, W), f32),
        pltpu.VMEM((2, C, CELLS), bf16),
        pltpu.VMEM((2, CH, 2 * C, W), f32),
        pltpu.VMEM((2, CH, 2 * C, W), f32),
        pltpu.VMEM((2, CH, C, W), f32),
        pltpu.VMEM((2, CH, C, W), f32),
        pltpu.VMEM((2, CH, C, W), f32),
        pltpu.VMEM((2, CH, 1, W), f32),
        pltpu.VMEM((2, C, CELLS), bf16),
        pltpu.VMEM((CH, C, W), bf16),
        pltpu.VMEM((CH, C, W), bf16),
        pltpu.VMEM((CH, C, W), bf16),
        pltpu.VMEM((2, C, CELLS), bf16),
        pltpu.VMEM((2, 5 * C, CELLS), bf16),
        pltpu.VMEM((2, 2, 8, N, N), bf16),
        pltpu.VMEM((8, N, N), bf16),
        pltpu.VMEM((3, N * 8, C), f32),
        pltpu.VMEM((3, N * 8, C), f32),
        pltpu.VMEM((2, CH // 2, D, 16, W), bf16),
        pltpu.VMEM((CH // 2, D, 16, W), bf16),
        pltpu.VMEM((4, 2, CH // 2, D, 16, W), bf16),
        pltpu.VMEM((4, CH // 2, D, 16, W), bf16),
        pltpu.VMEM((D, EARLY // D, C), bf16),
        pltpu.VMEM((D, LATE // D, C), bf16),
        pltpu.VMEM((D, EARLY // D, C), bf16),
        pltpu.VMEM((D, LATE // D, C), bf16),
        pltpu.VMEM((2, EARLY // D // 2, C), f32),
        pltpu.VMEM((2, EARLY // D // 2, C), f32),
        pltpu.VMEM((2, EARLY // D // 2, C), f32),
        pltpu.VMEM((nz, EARLY // D // 2, C), bf16),
        pltpu.VMEM((nz, LATE // D // 2, C), bf16),
        pltpu.VMEM((D, EARLY // D, C), bf16),
        pltpu.VMEM((D, LATE // D, C), bf16),
        pltpu.SemaphoreType.DMA((12, CH // 2)),
        pltpu.SemaphoreType.DMA((12, CH // 2)),
        pltpu.SemaphoreType.DMA((12, CH // 2)),
        pltpu.SemaphoreType.DMA((4,)),
        pltpu.SemaphoreType.DMA((4,)),
        pltpu.SemaphoreType.DMA((2,)),
        pltpu.SemaphoreType.DMA((4,)),
        pltpu.SemaphoreType.DMA((4,)),
        pltpu.SemaphoreType.DMA((2,)),
        pltpu.SemaphoreType.DMA((2,)),
    ]
    grad, in_total, out_total = pl.pallas_call(
        functools.partial(kernel, ndp),
        out_shape=(
            jax.ShapeDtypeStruct((R, N, C), bf16),
            jax.ShapeDtypeStruct((2, C, 5 * C), f32),
            jax.ShapeDtypeStruct((2, C, C), f32),
        ),
        in_specs=[vmem] * 5,
        out_specs=(vmem, vmem, vmem),
        scratch_shapes=scratch,
        compiler_params=pltpu.CompilerParams(
            collective_id=0, has_side_effects=True, vmem_limit_bytes=60 * 1024 * 1024
        ),
    )(pair[0], pair_cot[0], residue_mask, w_in, w_out)
    results = (grad, in_total, out_total)
    anywhere = pl.BlockSpec(memory_space=pltpu.HBM)
    grad, in_total, out_total = pl.pallas_call(
        hand_over,
        out_shape=tuple(jax.ShapeDtypeStruct(x.shape, x.dtype) for x in results),
        in_specs=[vmem] * 3,
        out_specs=(anywhere,) * 3,
        scratch_shapes=[pltpu.SemaphoreType.DMA((3,))],
    )(*results)
    return grad[None], in_total, out_total


def solution(mesh):
    return jax.shard_map(
        functools.partial(local, mesh.shape["dp"]),
        mesh=mesh,
        in_specs=(P("dp", "dap", None, None), P("dp", "dap", None, None), P("dp", None), P(), P()),
        out_specs=(P("dp", "dap", None, None), P(), P()),
        check_vma=False,
    )
```

```python
import functools

import jax
import jax.numpy as jnp
from jax import lax
from jax.experimental import pallas as pl
from jax.experimental.pallas import tpu as pltpu
from jax.sharding import PartitionSpec as P

EPS = 1e-05
D = 16
R = 12
N = 192
C = 128
CH = 6
W = 2 * N
CELLS = R * N
EARLY = 8 * C
LATE = 2 * C
FAR = (10, 6, 9, 11, 14, 2, 8, 5, 7, 13, 15, 1, 4, 3, 12)
f32 = jnp.float32
bf16 = jnp.bfloat16
MESH = pl.DeviceIdType.MESH


def dot(a, b, ca, cb):
    return lax.dot_general(a, b, (((ca,), (cb,)), ((), ())), preferred_element_type=f32)


def sigmoid(x):
    return 0.5 * jnp.tanh(0.5 * x) + 0.5


def normal_form(x):
    centred = x - jnp.mean(x, 0, keepdims=True)
    inv = lax.rsqrt(jnp.mean(centred * centred, 0, keepdims=True) + EPS)
    return centred * inv, inv


def norm_back(d, n, inv):
    return inv * (d - jnp.mean(d, 0, keepdims=True) - n * jnp.mean(d * n, 0, keepdims=True))


def kernel(
    ndp,
    pair_ref, cot_ref, mask_ref, win_ref, wo_ref,
    out_ref, gin_ref, gout_ref,
    wt_ref, wp_ref, wot_ref,
    n_ref, inv_ref, z_ref, v_ref, sg_ref, gate_ref, res_ref, ntri_ref, itri_ref, xz_ref,
    pt_ref, ct_ref, up_ref, dres_ref, dq_ref, lm_ref, tm_ref, a_ref, b_ref,
    big_send, small_send, big_recv, small_recv,
    early, mid, late, early_in, mid_in, late_in, half_mine, half_out, half_in,
    z_early, z_mid, z_late, early_all, mid_all, late_all,
    ssem, rsem, lsem, gs, gr, own, core_s, core_r, zs, zr,
):
    me = lax.axis_index("dap")
    my = lax.axis_index("dp")
    core, zed, nz = lax.rem(my, 2), my // 2, ndp // 2
    mate = my + 1 - 2 * core

    def offset(k, sign):
        j = k * 0
        for n, step in enumerate(FAR):
            j = jnp.where(k == n + 1, step, j)
        a, b = j // 4, lax.rem(j, 4)
        dx, dy = a + core * (b - a), b + core * (a - b)
        return lax.rem(me // 4 + 4 + sign * dx, 4) * 4 + lax.rem(lax.rem(me, 4) + 4 + sign * dy, 4)

    def peer_of(k):
        return offset(k, 1)

    def src_of(k):
        return offset(k, -1)

    def z_peer(k):
        return 2 * lax.rem(zed + k, nz) + core

    barrier = pltpu.get_barrier_semaphore()

    @pl.loop(1, D)
    def _(k):
        pl.semaphore_signal(barrier, inc=1, device_id={"dap": peer_of(k)}, device_id_type=MESH)

    pl.semaphore_signal(barrier, inc=1, device_id={"dp": mate}, device_id_type=MESH)

    @pl.loop(1, nz)
    def _(k):
        pl.semaphore_signal(barrier, inc=1, device_id={"dp": z_peer(k)}, device_id_type=MESH)

    def order_weights(u):
        wt = jnp.transpose(win_ref[u].astype(f32))
        pieces = []
        for t in range(2):
            left, right = (wt[(2 * e + t) * C : (2 * e + t + 1) * C].reshape(D, 8, C) for e in range(2))
            for g in range(2):
                at = slice(4 * g, 4 * g + 4)
                pieces.append(jnp.concatenate([left[:, at], right[:, at]], 1).reshape(C, C))
        wt_ref[u] = jnp.concatenate(pieces + [wt[4 * C : 5 * C]], 0).astype(bf16)

    def transpose_weights(u):
        wp_ref[u] = jnp.transpose(wt_ref[u].astype(f32)).astype(bf16)
        wot_ref[u] = jnp.transpose(wo_ref[u].astype(f32)).astype(bf16)

    order_weights(0)
    count = jnp.sum(mask_ref[...].astype(f32), 1, keepdims=True)

    def cell_mask(c):
        lane = lax.broadcasted_iota(jnp.int32, (1, W), 1)
        second = ((lane >= C) & (lane < 2 * C)) | (lane >= 2 * C + 64)
        k = jnp.where(lane < C, lane, jnp.where(lane < 2 * C + 64, lane - C, lane - N))
        k = jnp.where((lane >= C) & (lane < 2 * C), lane - C, k)
        row = me * R + 2 * c + second.astype(jnp.int32)
        return jnp.where((jnp.maximum(k, row).astype(f32) < count), 1.0, 0.0).astype(f32)

    def cells(c):
        return pl.ds(pl.multiple_of(c * W, C), W)

    def load_cells(ref, c):
        i = 2 * c
        x = jnp.concatenate(
            [ref[i, 0:C], ref[i + 1, 0:C], ref[i, C:N], ref[i + 1, C:N]], 0
        )
        return jnp.transpose(x.astype(f32))

    def part_copy(send, recv, phase, p, peer, slot):
        return pltpu.make_async_remote_copy(
            src_ref=send.at[p, peer], dst_ref=recv.at[p, slot],
            send_sem=ssem.at[phase, p], recv_sem=rsem.at[phase, p],
            device_id={"dap": peer}, device_id_type=MESH,
        )

    def own_copy(send, recv, phase, p):
        return pltpu.make_async_copy(send.at[p, me], recv.at[p, me], lsem.at[phase, p])

    def others(send, recv, phase, p):
        rest = pl.ds(0, D - 1)
        return pltpu.make_async_remote_copy(
            src_ref=send.at[p, rest], dst_ref=recv.at[p, rest],
            send_sem=ssem.at[phase, p], recv_sem=rsem.at[phase, p],
            device_id={"dap": peer_of(1)}, device_id_type=MESH,
        )

    def send_part(send, recv, phase, p):
        own_copy(send, recv, phase, p).start()

        @pl.loop(1, D)
        def _(k):
            part_copy(send, recv, phase, p, peer_of(k), me).start()

    def wait_part(send, recv, phase, p):
        own_copy(send, recv, phase, p).wait()
        others(send, recv, phase, p).wait_recv()

    def wait_sends(send, recv, phase):
        for p in range(CH // 2):
            others(send, recv, phase, p).wait_send()

    def normalize(u, c, x):
        n, inv = normal_form(x)
        n_ref[u, c] = n
        inv_ref[u, c] = inv
        z_ref[u, :, cells(c)] = n.astype(bf16)

    def factors_of(u, c, g):
        z = z_ref[u, :, cells(c)]
        v = dot(wt_ref[u, g * C : (g + 1) * C], z, 1, 0)
        sg = sigmoid(dot(wt_ref[u, (2 + g) * C : (3 + g) * C], z, 1, 0))
        v_ref[u, c, g * C : (g + 1) * C] = v
        sg_ref[u, c, g * C : (g + 1) * C] = sg
        return sg * v * cell_mask(c)

    def second_group(u, send, recv, phase):
        @pl.loop(0, CH // 2)
        def _(p):
            put_halves(send, p, [factors_of(u, 2 * p + a, 1) for a in range(2)])
            send_part(send, recv, phase, p)
            for a in range(2):
                c = 2 * p + a
                gate_ref[u, c] = sigmoid(dot(wt_ref[u, 4 * C : 5 * C], z_ref[u, :, cells(c)], 1, 0))

    def finish_product(u, c, t):
        n, inv = normal_form(t)
        ntri_ref[u, c] = n
        itri_ref[u, c] = inv
        xz = n.astype(bf16)
        xz_ref[u, :, cells(c)] = xz
        res = dot(wot_ref[u], xz, 1, 0)
        res_ref[u, c] = res
        return res

    def back_to_product(u, c, up):
        gate = gate_ref[u, c]
        dres = (up * gate).astype(bf16)
        dres_ref[u, :, cells(c)] = dres
        dq_ref[u, 4 * C : 5 * C, cells(c)] = (up * res_ref[u, c] * gate * (1.0 - gate)).astype(bf16)
        return norm_back(dot(wo_ref[u], dres, 1, 0), ntri_ref[u, c], itri_ref[u, c])

    def back_to_factors(u, p, g, slot):
        for a, d in enumerate(halves(big_recv.at[slot, g], p)):
            c = 2 * p + a
            sg = sg_ref[u, c, g * C : (g + 1) * C]
            dv = d * sg * cell_mask(c)
            dq_ref[u, g * C : (g + 1) * C, cells(c)] = dv.astype(bf16)
            dg = dv * v_ref[u, c, g * C : (g + 1) * C] * (1.0 - sg)
            dq_ref[u, (2 + g) * C : (3 + g) * C, cells(c)] = dg.astype(bf16)

    def back_to_pair(u, c):
        d = dot(wp_ref[u], dq_ref[u, :, cells(c)], 1, 0)
        return norm_back(d, n_ref[u, c], inv_ref[u, c])

    def halves(ref, p):
        x = ref[p].astype(f32).reshape(D, 2, 8, W)
        return x[:, 0].reshape(C, W), x[:, 1].reshape(C, W)

    def put_halves(ref, p, pieces):
        both = [y.reshape(D, 1, 8, W) for y in pieces]
        ref[p] = jnp.concatenate(both, 1).reshape(D, 16, W).astype(bf16)

    def put_rows(ref, at, x):
        rows = ref.shape[1]
        x = x.astype(bf16)
        for k in range(x.shape[0] // 16):
            r = at + 16 * k
            ref[r // rows, r % rows : r % rows + 16] = x[16 * k : 16 * k + 16]

    def out_grad(u):
        return dot(xz_ref[u], dres_ref[u], 1, 1)

    def spread(q, x, row):
        a_ref[q, pl.ds(row, 8)] = x[:, 0:C]
        a_ref[q, pl.ds(row + 8, 8)] = x[:, C : 2 * C]
        tail = x[:, 2 * C : W]
        b_ref[q, pl.ds(row, 8)] = tail
        b_ref[q, pl.ds(row + 8, 8)] = pltpu.roll(tail, 64, 1)

    def collect(q, row):
        lane = lax.broadcasted_iota(jnp.int32, (8, C), 1)
        tail = jnp.where(lane < 64, b_ref[q, pl.ds(row, 8)], b_ref[q, pl.ds(row + 8, 8)])
        return jnp.concatenate([a_ref[q, pl.ds(row, 8)], a_ref[q, pl.ds(row + 8, 8)], tail], 1)

    def get_channel(q, ch):
        a = a_ref[q, pl.ds(ch, N, stride=8), :]
        b = b_ref[q, pl.ds(ch, N, stride=8), :]
        return a.astype(bf16), b[:, :64].astype(bf16)

    def put_channel(q, ch, x):
        a_ref[q, pl.ds(ch, N, stride=8), :] = x[:, 0:C]
        b_ref[q, pl.ds(ch, N, stride=8), :] = jnp.concatenate([x[:, C:N], x[:, C:N]], 1)

    def unpack(q, send, recv, phase):
        for p in range(CH // 2):
            wait_part(send, recv, phase, p)

            @pl.loop(0, D)
            def _(k):
                x = recv[p, k].astype(f32)
                row = (k * R + 4 * p) * 8
                spread(q, x[0:8], row)
                spread(q, x[8:16], row + 16)

    def pack(q, send, recv, phase):
        @pl.loop(0, CH // 2)
        def _(p):
            @pl.loop(0, D)
            def _(k):
                row = (k * R + 4 * p) * 8
                send[p, k] = jnp.concatenate([collect(q, row), collect(q, row + 16)], 0).astype(bf16)

            send_part(send, recv, phase, p)

    def products(u, phase, slot):
        for g in range(2):
            unpack(g, big_send.at[g], big_recv.at[slot, g], phase + g)
            for ch in range(8):
                a, b = get_channel(g, ch)
                lm_ref[u, g, ch, :, 0:C] = a
                lm_ref[u, g, ch, :, C:N] = b
            for e in range(4):
                axis = 1 - u
                put_channel(2, 4 * g + e, dot(lm_ref[u, g, e], lm_ref[u, g, 4 + e], axis, axis))
        pack(2, small_send, small_recv.at[slot], phase + 2)

    def product_grads(u, phase, slot):
        unpack(2, small_send, small_recv.at[slot], phase)
        for g in range(2):
            for ch in range(4 * g, 4 * g + 4):
                a, b = get_channel(2, ch)
                tm_ref[ch, :, 0:C] = a
                tm_ref[ch, :, C:N] = b
            for e in range(4):
                left, right, grad = lm_ref[u, g, e], lm_ref[u, g, 4 + e], tm_ref[4 * g + e]
                if u == 0:
                    dleft, dright = dot(grad, right, 1, 0), dot(grad, left, 0, 0)
                else:
                    dleft, dright = dot(right, grad, 1, 1), dot(left, grad, 1, 0)
                put_channel(g, e, dleft)
                put_channel(g, 4 + e, dright)
            pack(g, big_send.at[g], big_recv.at[slot, g], phase + 1 + g)

    def sum_copy(rows, arrived, n, peer, slot, dev=None):
        return pltpu.make_async_remote_copy(
            src_ref=rows.at[peer], dst_ref=arrived.at[slot], send_sem=gs.at[n], recv_sem=gr.at[n],
            device_id={"dap": peer if dev is None else dev}, device_id_type=MESH,
        )

    def own_rows(rows, arrived, n):
        return pltpu.make_async_copy(rows.at[me], arrived.at[me], own.at[n])

    def start_sum(rows, arrived, n):
        own_rows(rows, arrived, n).start()

        @pl.loop(1, D)
        def _(k):
            sum_copy(rows, arrived, n, peer_of(k), me).start()

    def mate_copy(src, dst, n):
        return pltpu.make_async_remote_copy(
            src_ref=src, dst_ref=dst, send_sem=core_s.at[n], recv_sem=core_r.at[n],
            device_id={"dp": mate}, device_id_type=MESH,
        )

    def z_copy(zbuf, n, peer, slot):
        return pltpu.make_async_remote_copy(
            src_ref=zbuf.at[slot], dst_ref=zbuf.at[slot],
            send_sem=zs.at[n], recv_sem=zr.at[n],
            device_id={"dp": peer}, device_id_type=MESH,
        )

    def round_copy(everyone, n, peer, slot):
        return pltpu.make_async_remote_copy(
            src_ref=everyone.at[slot], dst_ref=everyone.at[slot],
            send_sem=gs.at[3 + n], recv_sem=gr.at[3 + n],
            device_id={"dap": peer}, device_id_type=MESH,
        )

    rest = pl.ds(0, D - 1)
    rest_z = pl.ds(0, nz - 1)

    def shared(rows, n):
        return rows.shape[1] // 2 if n == 0 else rows.shape[1]

    def own_half(rows):
        half = rows.shape[1] // 2
        return pl.ds(pl.multiple_of(core * half, half), half)

    def swap_rows(rows, n):
        at = pl.ds(0, shared(rows, n))
        return mate_copy(half_out.at[n, at], half_in.at[n, at], n)

    def sum_over_dap(rows, arrived, n):
        own_rows(rows, arrived, n).wait()
        sum_copy(rows, arrived, n, rest, rest, peer_of(1)).wait_recv()
        total = arrived[0].astype(f32)
        for k in range(1, D):
            total = total + arrived[k].astype(f32)
        mine, theirs = total, total
        size = shared(rows, n)
        if n == 0:
            mine = jnp.where(core == 0, total[:size], total[size:])
            theirs = jnp.where(core == 0, total[size:], total[:size])
        half_mine[n, 0:size] = mine
        half_out[n, 0:size] = theirs
        swap_rows(rows, n).start()

    def send_along_z(rows, zbuf, n):
        size = shared(rows, n)
        swap_rows(rows, n).wait_recv()
        zbuf[zed] = (half_mine[n, 0:size] + half_in[n, 0:size]).astype(bf16)

        @pl.loop(1, nz)
        def _(k):
            z_copy(zbuf, n, z_peer(k), zed).start()

    def hand_round(rows, zbuf, everyone, n):
        if nz > 1:
            z_copy(zbuf, n, z_peer(1), rest_z).wait_recv()

        total = zbuf[0].astype(f32)
        for k in range(1, nz):
            total = total + zbuf[k].astype(f32)
        total = total.astype(bf16)
        if n == 0:
            mine = own_half(rows)
            everyone[me, mine] = total
            back = mate_copy(everyone.at[me, mine], everyone.at[me, mine], 3)
            back.start()
            back.wait_recv()
        else:
            everyone[me] = total

        @pl.loop(1, D)
        def _(k):
            round_copy(everyone, n, peer_of(k), me).start()

    def end_sum(rows, arrived, zbuf, everyone, n):
        sum_copy(rows, arrived, n, rest, rest, peer_of(1)).wait_send()
        round_copy(everyone, n, peer_of(1), rest).wait_send()
        swap_rows(rows, n).wait_send()
        if n == 0:
            mate_copy(everyone.at[me, own_half(rows)], everyone.at[me, own_half(rows)], 3).wait_send()
        if nz > 1:
            z_copy(zbuf, n, z_peer(1), rest_z).wait_send()

    def big(slot, g):
        return big_send.at[g], big_recv.at[slot, g]

    def small(slot):
        return small_send, small_recv.at[slot]

    for p in range(CH // 2):
        pieces = []
        for a in range(2):
            c = 2 * p + a
            x = load_cells(pair_ref, c)
            pt_ref[c] = x.astype(bf16)
            normalize(0, c, x)
            pieces.append(factors_of(0, c, 0))
        put_halves(big_send.at[0], p, pieces)
        if p == 0:
            pl.semaphore_wait(barrier, D - 1 + nz)
        send_part(*big(0, 0), 0, p)
    second_group(0, *big(0, 1), 1)
    order_weights(1)
    transpose_weights(0)
    transpose_weights(1)
    products(0, 0, 0)
    wait_sends(*big(0, 0), 0)
    wait_sends(*big(0, 1), 1)

    @pl.loop(0, CH // 2)
    def _(p):
        wait_part(*small(0), 2, p)
        pieces = []
        for a, t in enumerate(halves(small_recv.at[0], p)):
            c = 2 * p + a
            res = finish_product(0, c, t)
            one = (pt_ref[c].astype(f32) + gate_ref[0, c] * res).astype(bf16)
            normalize(1, c, one.astype(f32))
            pieces.append(factors_of(1, c, 0))
        put_halves(big_send.at[0], p, pieces)
        send_part(*big(1, 0), 3, p)

    second_group(1, *big(1, 1), 4)
    wait_sends(*small(0), 2)

    @pl.loop(0, CH)
    def _(c):
        ct_ref[c] = load_cells(cot_ref, c).astype(bf16)

    products(1, 3, 1)
    wait_sends(*big(1, 0), 3)
    wait_sends(*big(1, 1), 4)
    wait_sends(*small(1), 5)

    @pl.loop(0, CH // 2)
    def _(p):
        wait_part(*small(1), 5, p)
        pieces = []
        for a, t in enumerate(halves(small_recv.at[1], p)):
            c = 2 * p + a
            finish_product(1, c, t)
            pieces.append(back_to_product(1, c, ct_ref[c].astype(f32)))
        put_halves(small_send, p, pieces)
        send_part(*small(2), 6, p)

    put_rows(early, 5 * C, out_grad(1))
    put_rows(early, 4 * C, dot(dq_ref[1, 4 * C : 5 * C], z_ref[1], 1, 1))
    product_grads(1, 6, 2)
    wait_sends(*small(2), 6)

    @pl.loop(0, CH // 2)
    def _(p):
        wait_part(*big(2, 0), 7, p)
        back_to_factors(1, p, 0, 2)

    for t in range(2):
        put_rows(early, 2 * t * C, dot(dq_ref[1, 2 * t * C : (2 * t + 1) * C], z_ref[1], 1, 1))

    @pl.loop(0, CH // 2)
    def _(p):
        wait_part(*big(2, 1), 8, p)
        back_to_factors(1, p, 1, 2)
        pieces = []
        for a in range(2):
            c = 2 * p + a
            up = (ct_ref[c].astype(f32) + back_to_pair(1, c)).astype(bf16)
            up_ref[c] = up
            pieces.append(back_to_product(0, c, up.astype(f32)))
        put_halves(small_send, p, pieces)
        send_part(*small(3), 9, p)

    for t in range(2):
        r = (2 * t + 1) * C
        put_rows(early, r, dot(dq_ref[1, r : r + C], z_ref[1], 1, 1))
    put_rows(early, 6 * C, out_grad(0))
    put_rows(early, 7 * C, dot(dq_ref[0, 4 * C : 5 * C], z_ref[0], 1, 1))
    start_sum(early, early_in, 0)
    wait_sends(*big(2, 0), 7)
    wait_sends(*big(2, 1), 8)
    product_grads(0, 9, 3)
    wait_sends(*small(3), 9)
    sum_over_dap(early, early_in, 0)

    @pl.loop(0, CH // 2)
    def _(p):
        wait_part(*big(3, 0), 10, p)
        back_to_factors(0, p, 0, 3)

    send_along_z(early, z_early, 0)
    put_rows(mid, 0, dot(dq_ref[0, 0:C], z_ref[0], 1, 1))
    put_rows(mid, C, dot(dq_ref[0, 2 * C : 3 * C], z_ref[0], 1, 1))
    start_sum(mid, mid_in, 1)

    @pl.loop(0, CH // 2)
    def _(p):
        wait_part(*big(3, 1), 11, p)
        back_to_factors(0, p, 1, 3)

    put_rows(late, 0, dot(dq_ref[0, C : 2 * C], z_ref[0], 1, 1))
    put_rows(late, C, dot(dq_ref[0, 3 * C : 4 * C], z_ref[0], 1, 1))
    start_sum(late, late_in, 2)
    sum_over_dap(mid, mid_in, 1)

    @pl.loop(0, CH)
    def _(c):
        total = up_ref[c].astype(f32) + back_to_pair(0, c)
        y = jnp.transpose(total).astype(bf16)
        i = 2 * c
        out_ref[i, 0:C] = y[0:C]
        out_ref[i + 1, 0:C] = y[C : 2 * C]
        out_ref[i, C:N] = y[2 * C : 2 * C + 64]
        out_ref[i + 1, C:N] = y[2 * C + 64 : W]

    send_along_z(mid, z_mid, 1)
    sum_over_dap(late, late_in, 2)
    send_along_z(late, z_late, 2)
    wait_sends(*big(3, 0), 10)
    wait_sends(*big(3, 1), 11)
    hand_round(early, z_early, early_all, 0)
    hand_round(mid, z_mid, mid_all, 1)
    hand_round(late, z_late, late_all, 2)

    def factors(x):
        blocks = []
        for e in range(2):
            for t in range(2):
                groups = [x[(2 * t + g) * C : (2 * t + g + 1) * C].reshape(D, 8, C) for g in range(2)]
                part = jnp.concatenate([y[:, 4 * e : 4 * e + 4] for y in groups], 1)
                blocks.append(jnp.transpose(part.reshape(C, C)))
        return blocks

    round_copy(early_all, 0, peer_of(1), rest).wait_recv()
    first = early_all[...].astype(f32).reshape(EARLY, C) * (1.0 / N)
    for k, block in enumerate(factors(first[0 : 4 * C]) + [jnp.transpose(first[4 * C : 5 * C])]):
        gin_ref[1, :, k * C : (k + 1) * C] = block
    gin_ref[0, :, 4 * C : 5 * C] = jnp.transpose(first[7 * C : 8 * C])
    gout_ref[0] = first[6 * C : 7 * C]
    gout_ref[1] = first[5 * C : 6 * C]

    round_copy(mid_all, 1, peer_of(1), rest).wait_recv()
    round_copy(late_all, 2, peer_of(1), rest).wait_recv()
    groups = [x[...].astype(f32).reshape(LATE, C) * (1.0 / N) for x in (mid_all, late_all)]
    last = jnp.concatenate([x[t * C : (t + 1) * C] for t in range(2) for x in groups], 0)
    for k, block in enumerate(factors(last)):
        gin_ref[0, :, k * C : (k + 1) * C] = block

    end_sum(early, early_in, z_early, early_all, 0)
    end_sum(mid, mid_in, z_mid, mid_all, 1)
    end_sum(late, late_in, z_late, late_all, 2)


def hand_over(a, b, c, x, y, z, sems):
    copies = [pltpu.make_async_copy(s, t, sems.at[k]) for k, (s, t) in enumerate(((a, x), (b, y), (c, z)))]
    for copy in copies:
        copy.start()
    for copy in copies:
        copy.wait()


def local(ndp, pair, pair_cot, residue_mask, w_in, w_out):
    vmem = pl.BlockSpec(memory_space=pltpu.VMEM)
    nz = ndp // 2
    scratch = [
        pltpu.VMEM((2, 5 * C, C), bf16),
        pltpu.VMEM((2, C, 5 * C), bf16),
        pltpu.VMEM((2, C, C), bf16),
        pltpu.VMEM((2, CH, C, W), f32),
        pltpu.VMEM((2, CH, 1, W), f32),
        pltpu.VMEM((2, C, CELLS), bf16),
        pltpu.VMEM((2, CH, 2 * C, W), f32),
        pltpu.VMEM((2, CH, 2 * C, W), f32),
        pltpu.VMEM((2, CH, C, W), f32),
        pltpu.VMEM((2, CH, C, W), f32),
        pltpu.VMEM((2, CH, C, W), f32),
        pltpu.VMEM((2, CH, 1, W), f32),
        pltpu.VMEM((2, C, CELLS), bf16),
        pltpu.VMEM((CH, C, W), bf16),
        pltpu.VMEM((CH, C, W), bf16),
        pltpu.VMEM((CH, C, W), bf16),
        pltpu.VMEM((2, C, CELLS), bf16),
        pltpu.VMEM((2, 5 * C, CELLS), bf16),
        pltpu.VMEM((2, 2, 8, N, N), bf16),
        pltpu.VMEM((8, N, N), bf16),
        pltpu.VMEM((3, N * 8, C), f32),
        pltpu.VMEM((3, N * 8, C), f32),
        pltpu.VMEM((2, CH // 2, D, 16, W), bf16),
        pltpu.VMEM((CH // 2, D, 16, W), bf16),
        pltpu.VMEM((4, 2, CH // 2, D, 16, W), bf16),
        pltpu.VMEM((4, CH // 2, D, 16, W), bf16),
        pltpu.VMEM((D, EARLY // D, C), bf16),
        pltpu.VMEM((D, LATE // D, C), bf16),
        pltpu.VMEM((D, LATE // D, C), bf16),
        pltpu.VMEM((D, EARLY // D, C), bf16),
        pltpu.VMEM((D, LATE // D, C), bf16),
        pltpu.VMEM((D, LATE // D, C), bf16),
        pltpu.VMEM((3, EARLY // D // 2, C), f32),
        pltpu.VMEM((3, EARLY // D // 2, C), f32),
        pltpu.VMEM((3, EARLY // D // 2, C), f32),
        pltpu.VMEM((nz, EARLY // D // 2, C), bf16),
        pltpu.VMEM((nz, LATE // D, C), bf16),
        pltpu.VMEM((nz, LATE // D, C), bf16),
        pltpu.VMEM((D, EARLY // D, C), bf16),
        pltpu.VMEM((D, LATE // D, C), bf16),
        pltpu.VMEM((D, LATE // D, C), bf16),
        pltpu.SemaphoreType.DMA((12, CH // 2)),
        pltpu.SemaphoreType.DMA((12, CH // 2)),
        pltpu.SemaphoreType.DMA((12, CH // 2)),
        pltpu.SemaphoreType.DMA((6,)),
        pltpu.SemaphoreType.DMA((6,)),
        pltpu.SemaphoreType.DMA((3,)),
        pltpu.SemaphoreType.DMA((4,)),
        pltpu.SemaphoreType.DMA((4,)),
        pltpu.SemaphoreType.DMA((3,)),
        pltpu.SemaphoreType.DMA((3,)),
    ]
    grad, in_total, out_total = pl.pallas_call(
        functools.partial(kernel, ndp),
        out_shape=(
            jax.ShapeDtypeStruct((R, N, C), bf16),
            jax.ShapeDtypeStruct((2, C, 5 * C), f32),
            jax.ShapeDtypeStruct((2, C, C), f32),
        ),
        in_specs=[vmem] * 5,
        out_specs=(vmem, vmem, vmem),
        scratch_shapes=scratch,
        compiler_params=pltpu.CompilerParams(
            collective_id=0, has_side_effects=True, vmem_limit_bytes=60 * 1024 * 1024
        ),
    )(pair[0], pair_cot[0], residue_mask, w_in, w_out)
    results = (grad, in_total, out_total)
    anywhere = pl.BlockSpec(memory_space=pltpu.HBM)
    grad, in_total, out_total = pl.pallas_call(
        hand_over,
        out_shape=tuple(jax.ShapeDtypeStruct(x.shape, x.dtype) for x in results),
        in_specs=[vmem] * 3,
        out_specs=(anywhere,) * 3,
        scratch_shapes=[pltpu.SemaphoreType.DMA((3,))],
    )(*results)
    return grad[None], in_total, out_total


def solution(mesh):
    return jax.shard_map(
        functools.partial(local, mesh.shape["dp"]),
        mesh=mesh,
        in_specs=(P("dp", "dap", None, None), P("dp", "dap", None, None), P("dp", None), P(), P()),
        out_specs=(P("dp", "dap", None, None), P(), P()),
        check_vma=False,
    )
```

```python
import functools

import jax
import jax.numpy as jnp
from jax import lax
from jax.experimental import pallas as pl
from jax.experimental.pallas import tpu as pltpu
from jax.sharding import PartitionSpec as P

EPS = 1e-05
D = 16
R = 12
N = 192
C = 128
CH = 6
W = 2 * N
CELLS = R * N
EARLY = 8 * C
LATE = 2 * C
FAR = (10, 6, 9, 11, 14, 2, 8, 5, 7, 13, 15, 1, 4, 3, 12)
f32 = jnp.float32
bf16 = jnp.bfloat16
MESH = pl.DeviceIdType.MESH


def dot(a, b, ca, cb):
    return lax.dot_general(a, b, (((ca,), (cb,)), ((), ())), preferred_element_type=f32)


def sigmoid(x):
    return 0.5 * jnp.tanh(0.5 * x) + 0.5


def normal_form(x):
    centred = x - jnp.mean(x, 0, keepdims=True)
    inv = lax.rsqrt(jnp.mean(centred * centred, 0, keepdims=True) + EPS)
    return centred * inv, inv


def norm_back(d, n, inv):
    return inv * (d - jnp.mean(d, 0, keepdims=True) - n * jnp.mean(d * n, 0, keepdims=True))


def kernel(
    ndp,
    pair_ref, cot_ref, mask_ref, win_ref, wo_ref,
    out_ref, gin_ref, gout_ref,
    wt_ref, wp_ref, wot_ref,
    n_ref, inv_ref, z_ref, v_ref, sg_ref, gate_ref, res_ref, ntri_ref, itri_ref, xz_ref,
    pt_ref, ct_ref, up_ref, dres_ref, dq_ref, lm_ref, tm_ref, a_ref, b_ref,
    big_send, small_send, big_recv, small_recv,
    early, mid, late, early_in, mid_in, late_in, half_mine, half_out, half_in,
    z_early, z_mid, z_late, early_all, mid_all, late_all,
    ssem, rsem, lsem, gs, gr, own, core_s, core_r, zs, zr,
):
    me = lax.axis_index("dap")
    my = lax.axis_index("dp")
    core, zed, nz = lax.rem(my, 2), my // 2, ndp // 2
    mate = my + 1 - 2 * core

    def offset(k, sign):
        j = k * 0
        for n, step in enumerate(FAR):
            j = jnp.where(k == n + 1, step, j)
        a, b = j // 4, lax.rem(j, 4)
        dx, dy = a + core * (b - a), b + core * (a - b)
        return lax.rem(me // 4 + 4 + sign * dx, 4) * 4 + lax.rem(lax.rem(me, 4) + 4 + sign * dy, 4)

    def peer_of(k):
        return offset(k, 1)

    def src_of(k):
        return offset(k, -1)

    def z_peer(k):
        return 2 * lax.rem(zed + k, nz) + core

    barrier = pltpu.get_barrier_semaphore()

    @pl.loop(1, D)
    def _(k):
        pl.semaphore_signal(barrier, inc=1, device_id={"dap": peer_of(k)}, device_id_type=MESH)

    pl.semaphore_signal(barrier, inc=1, device_id={"dp": mate}, device_id_type=MESH)

    @pl.loop(1, nz)
    def _(k):
        pl.semaphore_signal(barrier, inc=1, device_id={"dp": z_peer(k)}, device_id_type=MESH)

    def order_weights(u):
        wt = jnp.transpose(win_ref[u].astype(f32))
        pieces = []
        for t in range(2):
            left, right = (wt[(2 * e + t) * C : (2 * e + t + 1) * C].reshape(D, 8, C) for e in range(2))
            for g in range(2):
                at = slice(4 * g, 4 * g + 4)
                pieces.append(jnp.concatenate([left[:, at], right[:, at]], 1).reshape(C, C))
        wt_ref[u] = jnp.concatenate(pieces + [wt[4 * C : 5 * C]], 0).astype(bf16)

    def transpose_weights(u):
        wp_ref[u] = jnp.transpose(wt_ref[u].astype(f32)).astype(bf16)
        wot_ref[u] = jnp.transpose(wo_ref[u].astype(f32)).astype(bf16)

    order_weights(0)
    count = jnp.sum(mask_ref[...].astype(f32), 1, keepdims=True)

    def cell_mask(c):
        lane = lax.broadcasted_iota(jnp.int32, (1, W), 1)
        second = ((lane >= C) & (lane < 2 * C)) | (lane >= 2 * C + 64)
        k = jnp.where(lane < C, lane, jnp.where(lane < 2 * C + 64, lane - C, lane - N))
        k = jnp.where((lane >= C) & (lane < 2 * C), lane - C, k)
        row = me * R + 2 * c + second.astype(jnp.int32)
        return jnp.where((jnp.maximum(k, row).astype(f32) < count), 1.0, 0.0).astype(f32)

    def cells(c):
        return pl.ds(pl.multiple_of(c * W, C), W)

    def load_cells(ref, c):
        i = 2 * c
        x = jnp.concatenate(
            [ref[i, 0:C], ref[i + 1, 0:C], ref[i, C:N], ref[i + 1, C:N]], 0
        )
        return jnp.transpose(x.astype(f32))

    def part_copy(send, recv, phase, p, peer, slot):
        return pltpu.make_async_remote_copy(
            src_ref=send.at[p, peer], dst_ref=recv.at[p, slot],
            send_sem=ssem.at[phase, p], recv_sem=rsem.at[phase, p],
            device_id={"dap": peer}, device_id_type=MESH,
        )

    def own_copy(send, recv, phase, p):
        return pltpu.make_async_copy(send.at[p, me], recv.at[p, me], lsem.at[phase, p])

    def others(send, recv, phase, p):
        rest = pl.ds(0, D - 1)
        return pltpu.make_async_remote_copy(
            src_ref=send.at[p, rest], dst_ref=recv.at[p, rest],
            send_sem=ssem.at[phase, p], recv_sem=rsem.at[phase, p],
            device_id={"dap": peer_of(1)}, device_id_type=MESH,
        )

    def send_part(send, recv, phase, p):
        own_copy(send, recv, phase, p).start()

        @pl.loop(1, D)
        def _(k):
            part_copy(send, recv, phase, p, peer_of(k), me).start()

    def wait_part(send, recv, phase, p):
        own_copy(send, recv, phase, p).wait()
        others(send, recv, phase, p).wait_recv()

    def wait_sends(send, recv, phase):
        for p in range(CH // 2):
            others(send, recv, phase, p).wait_send()

    def normalize(u, c, x):
        n, inv = normal_form(x)
        n_ref[u, c] = n
        inv_ref[u, c] = inv
        z_ref[u, :, cells(c)] = n.astype(bf16)

    def factors_of(u, c, g):
        z = z_ref[u, :, cells(c)]
        v = dot(wt_ref[u, g * C : (g + 1) * C], z, 1, 0)
        sg = sigmoid(dot(wt_ref[u, (2 + g) * C : (3 + g) * C], z, 1, 0))
        v_ref[u, c, g * C : (g + 1) * C] = v
        sg_ref[u, c, g * C : (g + 1) * C] = sg
        return sg * v * cell_mask(c)

    def second_group(u, send, recv, phase):
        @pl.loop(0, CH // 2)
        def _(p):
            put_halves(send, p, [factors_of(u, 2 * p + a, 1) for a in range(2)])
            send_part(send, recv, phase, p)
            for a in range(2):
                c = 2 * p + a
                gate_ref[u, c] = sigmoid(dot(wt_ref[u, 4 * C : 5 * C], z_ref[u, :, cells(c)], 1, 0))

    def finish_product(u, c, t):
        n, inv = normal_form(t)
        ntri_ref[u, c] = n
        itri_ref[u, c] = inv
        xz = n.astype(bf16)
        xz_ref[u, :, cells(c)] = xz
        res = dot(wot_ref[u], xz, 1, 0)
        res_ref[u, c] = res
        return res

    def back_to_product(u, c, up):
        gate = gate_ref[u, c]
        dres = (up * gate).astype(bf16)
        dres_ref[u, :, cells(c)] = dres
        dq_ref[u, 4 * C : 5 * C, cells(c)] = (up * res_ref[u, c] * gate * (1.0 - gate)).astype(bf16)
        return norm_back(dot(wo_ref[u], dres, 1, 0), ntri_ref[u, c], itri_ref[u, c])

    def back_to_factors(u, p, g, slot):
        for a, d in enumerate(halves(big_recv.at[slot, g], p)):
            c = 2 * p + a
            sg = sg_ref[u, c, g * C : (g + 1) * C]
            dv = d * sg * cell_mask(c)
            dq_ref[u, g * C : (g + 1) * C, cells(c)] = dv.astype(bf16)
            dg = dv * v_ref[u, c, g * C : (g + 1) * C] * (1.0 - sg)
            dq_ref[u, (2 + g) * C : (3 + g) * C, cells(c)] = dg.astype(bf16)

    def back_to_pair(u, c):
        d = dot(wp_ref[u], dq_ref[u, :, cells(c)], 1, 0)
        return norm_back(d, n_ref[u, c], inv_ref[u, c])

    def halves(ref, p):
        x = ref[p].astype(f32).reshape(D, 2, 8, W)
        return x[:, 0].reshape(C, W), x[:, 1].reshape(C, W)

    def put_halves(ref, p, pieces):
        both = [y.reshape(D, 1, 8, W) for y in pieces]
        ref[p] = jnp.concatenate(both, 1).reshape(D, 16, W).astype(bf16)

    def put_rows(ref, at, x):
        rows = ref.shape[1]
        x = x.astype(bf16)
        for k in range(x.shape[0] // 16):
            r = at + 16 * k
            ref[r // rows, r % rows : r % rows + 16] = x[16 * k : 16 * k + 16]

    def out_grad(u):
        return dot(xz_ref[u], dres_ref[u], 1, 1)

    def spread(q, x, row):
        a_ref[q, pl.ds(row, 8)] = x[:, 0:C]
        a_ref[q, pl.ds(row + 8, 8)] = x[:, C : 2 * C]
        tail = x[:, 2 * C : W]
        b_ref[q, pl.ds(row, 8)] = tail
        b_ref[q, pl.ds(row + 8, 8)] = pltpu.roll(tail, 64, 1)

    def collect(q, row):
        lane = lax.broadcasted_iota(jnp.int32, (8, C), 1)
        tail = jnp.where(lane < 64, b_ref[q, pl.ds(row, 8)], b_ref[q, pl.ds(row + 8, 8)])
        return jnp.concatenate([a_ref[q, pl.ds(row, 8)], a_ref[q, pl.ds(row + 8, 8)], tail], 1)

    def get_channel(q, ch):
        a = a_ref[q, pl.ds(ch, N, stride=8), :]
        b = b_ref[q, pl.ds(ch, N, stride=8), :]
        return a.astype(bf16), b[:, :64].astype(bf16)

    def put_channel(q, ch, x):
        a_ref[q, pl.ds(ch, N, stride=8), :] = x[:, 0:C]
        b_ref[q, pl.ds(ch, N, stride=8), :] = jnp.concatenate([x[:, C:N], x[:, C:N]], 1)

    def unpack(q, send, recv, phase):
        for p in range(CH // 2):
            wait_part(send, recv, phase, p)

            @pl.loop(0, D)
            def _(k):
                x = recv[p, k].astype(f32)
                row = (k * R + 4 * p) * 8
                spread(q, x[0:8], row)
                spread(q, x[8:16], row + 16)

    def pack(q, send, recv, phase):
        @pl.loop(0, CH // 2)
        def _(p):
            @pl.loop(0, D)
            def _(k):
                row = (k * R + 4 * p) * 8
                send[p, k] = jnp.concatenate([collect(q, row), collect(q, row + 16)], 0).astype(bf16)

            send_part(send, recv, phase, p)

    def products(u, phase, slot):
        for g in range(2):
            unpack(g, big_send.at[g], big_recv.at[slot, g], phase + g)
            for ch in range(8):
                a, b = get_channel(g, ch)
                lm_ref[u, g, ch, :, 0:C] = a
                lm_ref[u, g, ch, :, C:N] = b
            for e in range(4):
                axis = 1 - u
                put_channel(2, 4 * g + e, dot(lm_ref[u, g, e], lm_ref[u, g, 4 + e], axis, axis))
        pack(2, small_send, small_recv.at[slot], phase + 2)

    def product_grads(u, phase, slot):
        unpack(2, small_send, small_recv.at[slot], phase)
        for g in range(2):
            for ch in range(4 * g, 4 * g + 4):
                a, b = get_channel(2, ch)
                tm_ref[ch, :, 0:C] = a
                tm_ref[ch, :, C:N] = b
            for e in range(4):
                left, right, grad = lm_ref[u, g, e], lm_ref[u, g, 4 + e], tm_ref[4 * g + e]
                if u == 0:
                    dleft, dright = dot(grad, right, 1, 0), dot(grad, left, 0, 0)
                else:
                    dleft, dright = dot(right, grad, 1, 1), dot(left, grad, 1, 0)
                put_channel(g, e, dleft)
                put_channel(g, 4 + e, dright)
            pack(g, big_send.at[g], big_recv.at[slot, g], phase + 1 + g)

    def sum_copy(rows, arrived, n, peer, slot, dev=None):
        return pltpu.make_async_remote_copy(
            src_ref=rows.at[peer], dst_ref=arrived.at[slot], send_sem=gs.at[n], recv_sem=gr.at[n],
            device_id={"dap": peer if dev is None else dev}, device_id_type=MESH,
        )

    def own_rows(rows, arrived, n):
        return pltpu.make_async_copy(rows.at[me], arrived.at[me], own.at[n])

    def start_sum(rows, arrived, n):
        own_rows(rows, arrived, n).start()

        @pl.loop(1, D)
        def _(k):
            sum_copy(rows, arrived, n, peer_of(k), me).start()

    def mate_copy(src, dst, n):
        return pltpu.make_async_remote_copy(
            src_ref=src, dst_ref=dst, send_sem=core_s.at[n], recv_sem=core_r.at[n],
            device_id={"dp": mate}, device_id_type=MESH,
        )

    def z_copy(zbuf, n, peer, slot):
        return pltpu.make_async_remote_copy(
            src_ref=zbuf.at[slot], dst_ref=zbuf.at[slot],
            send_sem=zs.at[n], recv_sem=zr.at[n],
            device_id={"dp": peer}, device_id_type=MESH,
        )

    def round_copy(everyone, n, peer, slot):
        return pltpu.make_async_remote_copy(
            src_ref=everyone.at[slot], dst_ref=everyone.at[slot],
            send_sem=gs.at[3 + n], recv_sem=gr.at[3 + n],
            device_id={"dap": peer}, device_id_type=MESH,
        )

    rest = pl.ds(0, D - 1)
    rest_z = pl.ds(0, nz - 1)

    def shared(rows, n):
        return rows.shape[1] // 2 if n == 0 else rows.shape[1]

    def own_half(rows):
        half = rows.shape[1] // 2
        return pl.ds(pl.multiple_of(core * half, half), half)

    def swap_rows(rows, n):
        at = pl.ds(0, shared(rows, n))
        return mate_copy(half_out.at[n, at], half_in.at[n, at], n)

    def sum_over_dap(rows, arrived, n):
        own_rows(rows, arrived, n).wait()
        sum_copy(rows, arrived, n, rest, rest, peer_of(1)).wait_recv()
        total = arrived[0].astype(f32)
        for k in range(1, D):
            total = total + arrived[k].astype(f32)
        mine, theirs = total, total
        size = shared(rows, n)
        if n == 0:
            mine = jnp.where(core == 0, total[:size], total[size:])
            theirs = jnp.where(core == 0, total[size:], total[:size])
        half_mine[n, 0:size] = mine
        half_out[n, 0:size] = theirs
        swap_rows(rows, n).start()

    def send_along_z(rows, zbuf, n):
        size = shared(rows, n)
        swap_rows(rows, n).wait_recv()
        zbuf[zed] = (half_mine[n, 0:size] + half_in[n, 0:size]).astype(bf16)

        @pl.loop(1, nz)
        def _(k):
            z_copy(zbuf, n, z_peer(k), zed).start()

    def hand_round(rows, zbuf, everyone, n):
        if nz > 1:
            z_copy(zbuf, n, z_peer(1), rest_z).wait_recv()

        total = zbuf[0].astype(f32)
        for k in range(1, nz):
            total = total + zbuf[k].astype(f32)
        total = total.astype(bf16)
        if n == 0:
            mine = own_half(rows)
            everyone[me, mine] = total
            back = mate_copy(everyone.at[me, mine], everyone.at[me, mine], 3)
            back.start()
            back.wait_recv()
        else:
            everyone[me] = total

        @pl.loop(1, D)
        def _(k):
            round_copy(everyone, n, peer_of(k), me).start()

    def end_sum(rows, arrived, zbuf, everyone, n):
        sum_copy(rows, arrived, n, rest, rest, peer_of(1)).wait_send()
        round_copy(everyone, n, peer_of(1), rest).wait_send()
        swap_rows(rows, n).wait_send()
        if n == 0:
            mate_copy(everyone.at[me, own_half(rows)], everyone.at[me, own_half(rows)], 3).wait_send()
        if nz > 1:
            z_copy(zbuf, n, z_peer(1), rest_z).wait_send()

    def big(slot, g):
        return big_send.at[g], big_recv.at[slot, g]

    def small(slot):
        return small_send, small_recv.at[slot]

    for p in range(CH // 2):
        pieces = []
        for a in range(2):
            c = 2 * p + a
            x = load_cells(pair_ref, c)
            pt_ref[c] = x.astype(bf16)
            normalize(0, c, x)
            pieces.append(factors_of(0, c, 0))
        put_halves(big_send.at[0], p, pieces)
        if p == 0:
            pl.semaphore_wait(barrier, D - 1 + nz)
        send_part(*big(0, 0), 0, p)
    second_group(0, *big(0, 1), 1)
    order_weights(1)
    transpose_weights(0)
    transpose_weights(1)
    products(0, 0, 0)
    wait_sends(*big(0, 0), 0)
    wait_sends(*big(0, 1), 1)

    @pl.loop(0, CH // 2)
    def _(p):
        wait_part(*small(0), 2, p)
        pieces = []
        for a, t in enumerate(halves(small_recv.at[0], p)):
            c = 2 * p + a
            res = finish_product(0, c, t)
            one = (pt_ref[c].astype(f32) + gate_ref[0, c] * res).astype(bf16)
            normalize(1, c, one.astype(f32))
            pieces.append(factors_of(1, c, 0))
        put_halves(big_send.at[0], p, pieces)
        send_part(*big(1, 0), 3, p)

    second_group(1, *big(1, 1), 4)
    wait_sends(*small(0), 2)

    @pl.loop(0, CH)
    def _(c):
        ct_ref[c] = load_cells(cot_ref, c).astype(bf16)

    products(1, 3, 1)
    wait_sends(*big(1, 0), 3)
    wait_sends(*big(1, 1), 4)
    wait_sends(*small(1), 5)

    @pl.loop(0, CH // 2)
    def _(p):
        wait_part(*small(1), 5, p)
        pieces = []
        for a, t in enumerate(halves(small_recv.at[1], p)):
            c = 2 * p + a
            finish_product(1, c, t)
            pieces.append(back_to_product(1, c, ct_ref[c].astype(f32)))
        put_halves(small_send, p, pieces)
        send_part(*small(2), 6, p)

    put_rows(early, 5 * C, out_grad(1))
    put_rows(early, 4 * C, dot(dq_ref[1, 4 * C : 5 * C], z_ref[1], 1, 1))
    product_grads(1, 6, 2)
    wait_sends(*small(2), 6)

    @pl.loop(0, CH // 2)
    def _(p):
        wait_part(*big(2, 0), 7, p)
        back_to_factors(1, p, 0, 2)

    for t in range(2):
        put_rows(early, 2 * t * C, dot(dq_ref[1, 2 * t * C : (2 * t + 1) * C], z_ref[1], 1, 1))

    @pl.loop(0, CH // 2)
    def _(p):
        wait_part(*big(2, 1), 8, p)
        back_to_factors(1, p, 1, 2)
        pieces = []
        for a in range(2):
            c = 2 * p + a
            up = (ct_ref[c].astype(f32) + back_to_pair(1, c)).astype(bf16)
            up_ref[c] = up
            pieces.append(back_to_product(0, c, up.astype(f32)))
        put_halves(small_send, p, pieces)
        send_part(*small(3), 9, p)

    for t in range(2):
        r = (2 * t + 1) * C
        put_rows(early, r, dot(dq_ref[1, r : r + C], z_ref[1], 1, 1))
    put_rows(early, 6 * C, out_grad(0))
    put_rows(early, 7 * C, dot(dq_ref[0, 4 * C : 5 * C], z_ref[0], 1, 1))
    start_sum(early, early_in, 0)
    wait_sends(*big(2, 0), 7)
    wait_sends(*big(2, 1), 8)
    product_grads(0, 9, 3)
    wait_sends(*small(3), 9)
    sum_over_dap(early, early_in, 0)

    @pl.loop(0, CH // 2)
    def _(p):
        wait_part(*big(3, 0), 10, p)
        back_to_factors(0, p, 0, 3)

    send_along_z(early, z_early, 0)
    put_rows(mid, 0, dot(dq_ref[0, 0:C], z_ref[0], 1, 1))
    put_rows(mid, C, dot(dq_ref[0, 2 * C : 3 * C], z_ref[0], 1, 1))
    start_sum(mid, mid_in, 1)

    @pl.loop(0, CH // 2)
    def _(p):
        wait_part(*big(3, 1), 11, p)
        back_to_factors(0, p, 1, 3)

    put_rows(late, 0, dot(dq_ref[0, C : 2 * C], z_ref[0], 1, 1))
    put_rows(late, C, dot(dq_ref[0, 3 * C : 4 * C], z_ref[0], 1, 1))
    start_sum(late, late_in, 2)
    sum_over_dap(mid, mid_in, 1)

    @pl.loop(0, CH)
    def _(c):
        total = up_ref[c].astype(f32) + back_to_pair(0, c)
        y = jnp.transpose(total).astype(bf16)
        i = 2 * c
        out_ref[i, 0:C] = y[0:C]
        out_ref[i + 1, 0:C] = y[C : 2 * C]
        out_ref[i, C:N] = y[2 * C : 2 * C + 64]
        out_ref[i + 1, C:N] = y[2 * C + 64 : W]

    send_along_z(mid, z_mid, 1)
    sum_over_dap(late, late_in, 2)
    send_along_z(late, z_late, 2)
    wait_sends(*big(3, 0), 10)
    wait_sends(*big(3, 1), 11)
    hand_round(early, z_early, early_all, 0)
    hand_round(mid, z_mid, mid_all, 1)
    hand_round(late, z_late, late_all, 2)

    def factors(x):
        blocks = []
        for e in range(2):
            for t in range(2):
                groups = [x[(2 * t + g) * C : (2 * t + g + 1) * C].reshape(D, 8, C) for g in range(2)]
                part = jnp.concatenate([y[:, 4 * e : 4 * e + 4] for y in groups], 1)
                blocks.append(jnp.transpose(part.reshape(C, C)))
        return blocks

    round_copy(early_all, 0, peer_of(1), rest).wait_recv()
    first = early_all[...].astype(f32).reshape(EARLY, C) * (1.0 / N)
    for k, block in enumerate(factors(first[0 : 4 * C]) + [jnp.transpose(first[4 * C : 5 * C])]):
        gin_ref[1, :, k * C : (k + 1) * C] = block
    gin_ref[0, :, 4 * C : 5 * C] = jnp.transpose(first[7 * C : 8 * C])
    gout_ref[0] = first[6 * C : 7 * C]
    gout_ref[1] = first[5 * C : 6 * C]

    round_copy(mid_all, 1, peer_of(1), rest).wait_recv()
    round_copy(late_all, 2, peer_of(1), rest).wait_recv()
    groups = [x[...].astype(f32).reshape(LATE, C) * (1.0 / N) for x in (mid_all, late_all)]
    last = jnp.concatenate([x[t * C : (t + 1) * C] for t in range(2) for x in groups], 0)
    for k, block in enumerate(factors(last)):
        gin_ref[0, :, k * C : (k + 1) * C] = block

    end_sum(early, early_in, z_early, early_all, 0)
    end_sum(mid, mid_in, z_mid, mid_all, 1)
    end_sum(late, late_in, z_late, late_all, 2)


def hand_over(a, b, c, x, y, z, sems):
    copies = [pltpu.make_async_copy(s, t, sems.at[k]) for k, (s, t) in enumerate(((a, x), (b, y), (c, z)))]
    for copy in copies:
        copy.start()
    for copy in copies:
        copy.wait()


def local(ndp, pair, pair_cot, residue_mask, w_in, w_out):
    vmem = pl.BlockSpec(memory_space=pltpu.VMEM)
    nz = ndp // 2
    scratch = [
        pltpu.VMEM((2, 5 * C, C), bf16),
        pltpu.VMEM((2, C, 5 * C), bf16),
        pltpu.VMEM((2, C, C), bf16),
        pltpu.VMEM((2, CH, C, W), f32),
        pltpu.VMEM((2, CH, 1, W), f32),
        pltpu.VMEM((2, C, CELLS), bf16),
        pltpu.VMEM((2, CH, 2 * C, W), f32),
        pltpu.VMEM((2, CH, 2 * C, W), f32),
        pltpu.VMEM((2, CH, C, W), f32),
        pltpu.VMEM((2, CH, C, W), f32),
        pltpu.VMEM((2, CH, C, W), f32),
        pltpu.VMEM((2, CH, 1, W), f32),
        pltpu.VMEM((2, C, CELLS), bf16),
        pltpu.VMEM((CH, C, W), bf16),
        pltpu.VMEM((CH, C, W), bf16),
        pltpu.VMEM((CH, C, W), bf16),
        pltpu.VMEM((2, C, CELLS), bf16),
        pltpu.VMEM((2, 5 * C, CELLS), bf16),
        pltpu.VMEM((2, 2, 8, N, N), bf16),
        pltpu.VMEM((8, N, N), bf16),
        pltpu.VMEM((3, N * 8 + 8, C), f32),
        pltpu.VMEM((3, N * 8 + 8, C), f32),
        pltpu.VMEM((2, CH // 2, D, 16, W), bf16),
        pltpu.VMEM((CH // 2, D, 16, W), bf16),
        pltpu.VMEM((4, 2, CH // 2, D, 16, W), bf16),
        pltpu.VMEM((4, CH // 2, D, 16, W), bf16),
        pltpu.VMEM((D, EARLY // D, C), bf16),
        pltpu.VMEM((D, LATE // D, C), bf16),
        pltpu.VMEM((D, LATE // D, C), bf16),
        pltpu.VMEM((D, EARLY // D, C), bf16),
        pltpu.VMEM((D, LATE // D, C), bf16),
        pltpu.VMEM((D, LATE // D, C), bf16),
        pltpu.VMEM((3, EARLY // D // 2, C), f32),
        pltpu.VMEM((3, EARLY // D // 2, C), f32),
        pltpu.VMEM((3, EARLY // D // 2, C), f32),
        pltpu.VMEM((nz, EARLY // D // 2, C), bf16),
        pltpu.VMEM((nz, LATE // D, C), bf16),
        pltpu.VMEM((nz, LATE // D, C), bf16),
        pltpu.VMEM((D, EARLY // D, C), bf16),
        pltpu.VMEM((D, LATE // D, C), bf16),
        pltpu.VMEM((D, LATE // D, C), bf16),
        pltpu.SemaphoreType.DMA((12, CH // 2)),
        pltpu.SemaphoreType.DMA((12, CH // 2)),
        pltpu.SemaphoreType.DMA((12, CH // 2)),
        pltpu.SemaphoreType.DMA((6,)),
        pltpu.SemaphoreType.DMA((6,)),
        pltpu.SemaphoreType.DMA((3,)),
        pltpu.SemaphoreType.DMA((4,)),
        pltpu.SemaphoreType.DMA((4,)),
        pltpu.SemaphoreType.DMA((3,)),
        pltpu.SemaphoreType.DMA((3,)),
    ]
    grad, in_total, out_total = pl.pallas_call(
        functools.partial(kernel, ndp),
        out_shape=(
            jax.ShapeDtypeStruct((R, N, C), bf16),
            jax.ShapeDtypeStruct((2, C, 5 * C), f32),
            jax.ShapeDtypeStruct((2, C, C), f32),
        ),
        in_specs=[vmem] * 5,
        out_specs=(vmem, vmem, vmem),
        scratch_shapes=scratch,
        compiler_params=pltpu.CompilerParams(
            collective_id=0, has_side_effects=True, vmem_limit_bytes=60 * 1024 * 1024
        ),
    )(pair[0], pair_cot[0], residue_mask, w_in, w_out)
    results = (grad, in_total, out_total)
    anywhere = pl.BlockSpec(memory_space=pltpu.HBM)
    grad, in_total, out_total = pl.pallas_call(
        hand_over,
        out_shape=tuple(jax.ShapeDtypeStruct(x.shape, x.dtype) for x in results),
        in_specs=[vmem] * 3,
        out_specs=(anywhere,) * 3,
        scratch_shapes=[pltpu.SemaphoreType.DMA((3,))],
    )(*results)
    return grad[None], in_total, out_total


def solution(mesh):
    return jax.shard_map(
        functools.partial(local, mesh.shape["dp"]),
        mesh=mesh,
        in_specs=(P("dp", "dap", None, None), P("dp", "dap", None, None), P("dp", None), P(), P()),
        out_specs=(P("dp", "dap", None, None), P(), P()),
        check_vma=False,
    )
```
